32 devices in a mesh: ctx: 8 (over z, y), head: 4 (over x, core).
Axes of the slice: x: 2, y: 2, z: 4, core: 2. Of those that a mesh axis runs over, the one named last changes fastest.
Arguments:
- query: bfloat16 [8, 2, 512, 4096], P('ctx', None, None, 'head'), may hold values from -48 to 48
- key: bfloat16 [8, 2, 512, 512], P('ctx', None, 'head'), may hold values from -18 to 18
- value: bfloat16 [8, 2, 512, 512], P('ctx', None, 'head'), may hold values from -6 to 6
- d_out: bfloat16 [8, 2, 512, 4096], P('ctx', None, None, 'head'), may hold values from -6 to 6
- doc_start: int32 [64], replicated, may hold values from 0 to 1, as said below
Outputs:
- d_query: bfloat16 [8, 2, 512, 4096], P('ctx', None, None, 'head')
- d_key: bfloat16 [8, 2, 512, 512], P('ctx', None, 'head')
- d_value: bfloat16 [8, 2, 512, 512], P('ctx', None, 'head')
The draws below stay inside these ranges and needn't reach their ends.
Inputs may be any that keep to these rules, and one draw needn't show every extreme that they name: `doc_start`: 1 where a document begins at that block of 128 tokens (blocks in sequence order); block 0 begins one; from every beginning the next beginning, or the end of the sequence, is 1 to 3 blocks away; the first block of every span after the first lies inside a document of exactly 3 blocks that began in the span before.
All inputs are finite; a program needn't handle non-finite values.
Results may differ from the reference program's by a relative error of at most 0.039.
Values may be sent and summed in bfloat16 or wider, within the bound.
No kernel may reach another device: no remote copies, remote signals or barrier semaphores. Data moves between devices by JAX's collectives and lax.ppermute only.
A program may use at most 64 MiB of HBM per device.

```python
import jax
import jax.numpy as jnp
from jax import lax

QH = 32
KVH = 4
HD = 128
BLK = 128
LMAX_BLK = 3
GROUP = 8
CH = 512
CHB = 4
NCHUNK = 16
S_BLK = 64
TAIL = 256
N_CTX = 8


def key_parts(key):
    common = jax.random.fold_in(key, 21)
    drawn = jax.random.truncated_normal(jax.random.fold_in(common, 3), -6.0, 6.0, (NCHUNK // 2, 2, CH, KVH * HD), jnp.float32)
    return drawn


def draw_key(key, part):
    drawn = key_parts(key)
    return drawn.astype(jnp.bfloat16)


def draw_query(key, part):
    own_key = jax.random.fold_in(key, 31)
    drawn_query = jax.random.truncated_normal(jax.random.fold_in(own_key, 4), -6.0, 6.0, (NCHUNK // 2, 2, CH, QH * HD), jnp.float32)
    return drawn_query.astype(jnp.bfloat16)


def draw_doc_start(key, part):
    gaps = jax.random.randint(jax.random.fold_in(key, 11), (S_BLK,), 1, LMAX_BLK + 1)
    beginnings = jnp.cumsum(gaps) - gaps
    positions = jnp.arange(S_BLK, dtype=jnp.int32)
    flags = jnp.any(beginnings[None, :] == positions[:, None], axis=1)
    span_ids = jnp.arange(1, NCHUNK, dtype=jnp.int32)
    backward = jax.random.randint(jax.random.fold_in(key, 13), (NCHUNK - 1,), 1, LMAX_BLK)
    openings = span_ids * CHB - backward
    closings = openings + LMAX_BLK
    inside = jnp.any((positions[:, None] > openings[None, :]) & (positions[:, None] < closings[None, :]), axis=1)
    endpoint = jnp.any((positions[:, None] == openings[None, :]) | (positions[:, None] == closings[None, :]), axis=1)
    flags = jnp.where(inside, False, flags)
    flags = jnp.where(endpoint, True, flags)
    return flags.astype(jnp.int32)


def steps_of(key, dims, split, low, largest):
    loudness, own = 1.0, jax.random.fold_in(key, 6)
    for axis_at, shards_of in split:
        heights = jnp.exp(jax.random.uniform(jax.random.fold_in(own, axis_at), (shards_of,), jnp.float32, low / len(split), largest / len(split)))
        loudness = loudness * jnp.repeat(heights, dims[axis_at] // shards_of).reshape([-1 if axis == axis_at else 1 for axis in range(len(dims))])
    return loudness


def noise(rng, extent, deviation, bound, cuts=(), held_as=jnp.bfloat16):
    factor_of = steps_of(rng, extent, cuts, -0.22, 0.18) if cuts else 1.0
    drawn = jax.random.normal(rng, extent, jnp.float32) * deviation * factor_of
    return jnp.minimum(jnp.maximum(drawn, -bound), bound).astype(held_as)


def setup_inputs(seed: int = 0) -> dict:
    streams_of = jax.random.split(jax.random.key(seed), 6)
    return {
        "query": draw_query(jax.random.fold_in(streams_of[5], 71), 0),
        "key": draw_key(jax.random.fold_in(streams_of[5], 71), 0),
        "value": noise(streams_of[2], (N_CTX, 2, CH, KVH * HD), 1.0, 6.0, ((0, 8), (2, 4))),
        "d_out": noise(streams_of[3], (N_CTX, 2, CH, QH * HD), 1.0, 6.0, ((0, 8), (3, 4))),
        "doc_start": draw_doc_start(jax.random.fold_in(streams_of[5], 71), 0),
    }


def unfolded(array):
    return jnp.concatenate([array[:, 0], array[::-1, 1]], axis=0)


def refolded(array):
    halves = array.shape[0] // 2
    return jnp.stack([array[:halves], array[halves:][::-1]], axis=1)


def rounded(values):
    return lax.optimization_barrier(values.astype(jnp.bfloat16)).astype(jnp.float32)


def windowed(extended):
    pieces = []
    for offset in range(LMAX_BLK):
        sliced = lax.slice_in_dim(extended, offset * BLK, offset * BLK + CH, axis=0)
        pieces.append(sliced.reshape((CHB, BLK) + extended.shape[1:]))
    return jnp.concatenate(pieces, axis=1)


def unwindowed(windows):
    summed = jnp.zeros((TAIL + CH,) + windows.shape[2:], jnp.float32)
    for offset in range(LMAX_BLK):
        sliced = windows[:, offset * BLK:(offset + 1) * BLK].reshape((CH,) + windows.shape[2:])
        summed = summed.at[offset * BLK:offset * BLK + CH].add(sliced)
    return summed


def span_terms(operands):
    queries, grads_out, keys_ext, values_ext, doc_begins, span_start = operands
    score_scale = HD ** -0.5
    q_blocks = queries.reshape(CHB, BLK, KVH, GROUP, HD).astype(jnp.float32)
    do_blocks = grads_out.reshape(CHB, BLK, KVH, GROUP, HD).astype(jnp.float32)
    k_windows = windowed(keys_ext).astype(jnp.float32)
    v_windows = windowed(values_ext).astype(jnp.float32)
    row_pos = jnp.arange(BLK, dtype=jnp.int32)[None, :, None]
    col_pos = jnp.arange(LMAX_BLK * BLK, dtype=jnp.int32)[None, None, :]
    key_pos = span_start - TAIL + jnp.arange(CHB, dtype=jnp.int32)[:, None, None] * BLK + col_pos
    visible = (col_pos <= row_pos + TAIL) & (key_pos >= doc_begins[:, None, None])
    visible = visible[:, None, None]
    scores = jnp.einsum('btgjd,bkgd->bgjtk', q_blocks, k_windows) * score_scale
    peak = jnp.max(jnp.where(visible, scores, -1e30), axis=-1, keepdims=True)
    weights = jnp.exp(jnp.where(visible, scores - peak, -1e30))
    probs = weights / jnp.sum(weights, axis=-1, keepdims=True)
    probs_b = rounded(probs)
    outputs = rounded(jnp.einsum('bgjtk,bkgd->btgjd', probs_b, v_windows))
    deltas = jnp.sum(do_blocks * outputs, axis=-1)
    dprobs = jnp.einsum('btgjd,bkgd->bgjtk', do_blocks, v_windows)
    dscores = rounded(probs * (dprobs - jnp.transpose(deltas, (0, 2, 3, 1))[..., None]) * score_scale)
    d_queries = jnp.einsum('bgjtk,bkgd->btgjd', dscores, k_windows).astype(jnp.bfloat16)
    dk_windows = jnp.einsum('bgjtk,btgjd->bkgd', dscores, q_blocks)
    dv_windows = jnp.einsum('bgjtk,btgjd->bkgd', probs_b, do_blocks)
    return (d_queries.reshape(CH, QH * HD),
            unwindowed(dk_windows).reshape(TAIL + CH, KVH * HD),
            unwindowed(dv_windows).reshape(TAIL + CH, KVH * HD))


def extended_lines(array):
    line = unfolded(array).reshape(NCHUNK, CH, KVH, HD)
    leading = jnp.concatenate([jnp.zeros((1, TAIL, KVH, HD), array.dtype), line[:-1, CH - TAIL:]], axis=0)
    return jnp.concatenate([leading, line], axis=1)


def reference(query, key, value, d_out, doc_start):
    line_q = unfolded(query)
    line_do = unfolded(d_out)
    ext_k = extended_lines(key)
    ext_v = extended_lines(value)
    run_begin = lax.cummax(jnp.where(doc_start == 1, jnp.arange(S_BLK, dtype=jnp.int32), 0), axis=0) * BLK
    begins = run_begin.reshape(NCHUNK, CHB)
    starts = jnp.arange(NCHUNK, dtype=jnp.int32) * CH
    line_dq, dk_ext, dv_ext = lax.map(span_terms, (line_q, line_do, ext_k, ext_v, begins, starts))
    dk_line = dk_ext[:, TAIL:].at[:-1, CH - TAIL:].add(dk_ext[1:, :TAIL])
    dv_line = dv_ext[:, TAIL:].at[:-1, CH - TAIL:].add(dv_ext[1:, :TAIL])
    d_query = refolded(line_dq)
    d_key = refolded(dk_line.astype(jnp.bfloat16))
    d_value = refolded(dv_line.astype(jnp.bfloat16))
    return d_query, d_key, d_value
```

```python
import functools

import jax
import jax.numpy as jnp
from jax import lax
from jax.experimental import pallas as pl
from jax.experimental.pallas import tpu as pltpu
from jax.sharding import PartitionSpec as P

HD = 128
BLK = 128
REACH = 2
SCALE = HD**-0.5
SCALE_LOG2E = SCALE * 1.4426950408889634
BF16 = jnp.bfloat16
F32 = jnp.float32
VMEM = pl.BlockSpec(memory_space=pltpu.VMEM)
SMEM = pl.BlockSpec(memory_space=pltpu.SMEM)


def shape(dims, dtype=BF16):
    return jax.ShapeDtypeStruct(dims, dtype)


def call(body, inputs, outs, scratch=(), flops=0, limit=12, out_spec=VMEM):
    in_specs = [SMEM if a.dtype == jnp.int32 else VMEM for a in inputs]
    size = sum(o.size * o.dtype.itemsize for o in outs)
    return pl.pallas_call(
        body,
        out_shape=outs,
        in_specs=in_specs,
        out_specs=[out_spec] * len(outs),
        scratch_shapes=list(scratch),
        compiler_params=pltpu.CompilerParams(vmem_limit_bytes=limit << 20),
        cost_estimate=pl.CostEstimate(flops=flops, bytes_accessed=size, transcendentals=0),
        name=body.func.__name__,
    )(*inputs)


def lanes(index):
    return pl.ds(pl.multiple_of(index * HD, HD), HD)


def rows(index, blocks=1):
    return pl.ds(pl.multiple_of(index * BLK, BLK), blocks * BLK)


def pack_keys(heads, place, key, value, *sends):
    me, first = place[0], place[1]
    for half in range(2):
        slot = first if half == 0 else 1 - first
        for t in range(1, heads):
            out = sends[half * (heads - 1) + t - 1]
            out[0] = key[0, slot, :, lanes(me ^ t)]
            out[1] = value[0, slot, :, lanes(me ^ t)]


def join_keys(heads, half, place, key, value, *refs):
    received, (span, rim) = refs[: heads - 1], refs[heads - 1 :]
    me = place[0]
    slot = place[1] if half == 0 else 1 - place[1]
    span[0, rows(me), :] = key[0, slot, :, lanes(me)]
    span[1, rows(me), :] = value[0, slot, :, lanes(me)]
    for t in range(1, heads):
        span[0, rows(me ^ t), :] = received[t - 1][0]
        span[1, rows(me ^ t), :] = received[t - 1][1]
    rim[...] = span[:, (heads - REACH) * BLK :, :]


def dot(a, b, ca, cb):
    return lax.dot_general(a, b, (((ca,), (cb,)), ((), ())), preferred_element_type=F32)


def block_grads(n, first, queries, grads, keys, d_queries, d_keys):
    count = queries.shape[1] // HD
    window = pl.ds(first * BLK, n * BLK)
    k, v = keys[0, window, :], keys[1, window, :]
    q = jnp.concatenate([queries[:, j * HD : (j + 1) * HD] for j in range(count)], axis=0)
    do = jnp.concatenate([grads[:, j * HD : (j + 1) * HD] for j in range(count)], axis=0)
    s = dot(k, q, 1, 1)
    dp = dot(v, do, 1, 1)
    token = lax.broadcasted_iota(jnp.int32, (BLK, count * BLK), 1) & (BLK - 1)
    seen = lax.broadcasted_iota(jnp.int32, (BLK, count * BLK), 0) <= token
    last = jnp.where(seen, s[(n - 1) * BLK :], -jnp.inf)
    s = jnp.concatenate([s[: (n - 1) * BLK], last], axis=0) if n > 1 else last
    peak = jnp.max(s, axis=0, keepdims=True)
    w = jnp.exp2((s - peak) * SCALE_LOG2E)
    inverse = 1.0 / jnp.sum(w, axis=0, keepdims=True)
    delta = jnp.sum(w * dp, axis=0, keepdims=True) * inverse
    p = w * inverse
    ds = (p * (dp - delta)).astype(BF16)
    d_keys[0, window, :] += dot(ds, q, 1, 0) * SCALE
    d_keys[1, window, :] += dot(p.astype(BF16), do, 1, 0)
    dq = (dot(k.T, ds, 1, 0) * SCALE).astype(BF16)
    for j in range(count):
        d_queries[:, j * HD : (j + 1) * HD] = dq[:, j * BLK : (j + 1) * BLK].T


def span_part(first_block, blocks, per_span, half, place, doc_start, query, d_out, keys, d_query, d_keys):
    slot = place[1] if half == 0 else 1 - place[1]
    span = place[3] if half == 0 else place[4]
    d_keys[...] = jnp.zeros_like(d_keys)
    for b in range(blocks):
        block = span * per_span + first_block + b
        here = doc_start[block]
        before = doc_start[jnp.maximum(block - 1, 0)]
        visible = jnp.where(here == 1, 1, jnp.where(before == 1, 2, 3))
        tokens = pl.ds((first_block + b) * BLK, BLK)
        for n in range(1, REACH + 2):

            @pl.when(visible == n)
            def _(n=n, tokens=tokens, b=b):
                block_grads(
                    n,
                    b + REACH + 1 - n,
                    query.at[0, slot, tokens, :],
                    d_out.at[0, slot, tokens, :],
                    keys,
                    d_query.at[pl.ds(b * BLK, BLK), :],
                    d_keys,
                )


def late_blocks(per_span, half, place, doc_start, query, d_out, keys, d_query, d_keys):
    span_part(REACH, per_span - REACH, per_span, half, place, doc_start, query, d_out, keys, d_query, d_keys)


def early_blocks(per_span, half, place, doc_start, query, d_out, keys, other, incoming, d_query, d_own, d_rim, window, d_window):
    cut = REACH * BLK
    window[:, cut:, :] = keys[:, :cut, :]
    window[:, :cut, :] = incoming[...]
    if half == 1:

        @pl.when(place[2] == 1)
        def _():
            window[:, :cut, :] = other[:, (per_span - REACH) * BLK :, :]

    span_part(0, REACH, per_span, half, place, doc_start, query, d_out, window, d_query, d_window)
    d_rim[...] = d_window[:, :cut, :].astype(BF16)
    d_own[...] = d_window[:, cut:, :]


def store_queries(reach, place, early_first, late_first, early_second, late_second, d_query, sems):
    copies = []
    for half, parts in ((0, (early_first, late_first)), (1, (early_second, late_second))):
        slot = place[1] if half == 0 else 1 - place[1]
        for part, start in zip(parts, (0, reach * BLK)):
            there = d_query.at[0, slot, pl.ds(start, part.shape[0]), :]
            copies.append(pltpu.make_async_copy(part, there, sems.at[len(copies)]))
    for copy in copies:
        copy.start()
    for copy in copies:
        copy.wait()


def pack_grads(heads, half, place, d_late, d_own, d_back, d_local, *refs):
    sends, total = refs[:-1], refs[-1]
    me = place[0]
    cut = REACH * BLK
    total[...] = d_late[...]
    total[:, :cut, :] += d_own[...]
    total[:, (heads - REACH) * BLK :, :] += d_back[...].astype(F32)
    if half == 0:

        @pl.when(place[2] == 1)
        def _():
            total[:, (heads - REACH) * BLK :, :] += d_local[...].astype(F32)

    for t in range(heads):
        sends[t][...] = total[:, rows(me ^ t), :].astype(BF16)


def join_grads(heads, place, *refs):
    parts, (d_key, d_value) = refs[: 2 * heads], refs[2 * heads :]
    me = place[0]
    for half in range(2):
        slot = place[1] if half == 0 else 1 - place[1]
        for t in range(heads):
            d_key[0, slot, :, lanes(me ^ t)] = parts[half * heads + t][0]
            d_value[0, slot, :, lanes(me ^ t)] = parts[half * heads + t][1]


def per_device(query, key, value, d_out, doc_start):
    ctx, ctx_count = lax.axis_index("ctx"), lax.axis_size("ctx")
    head, heads = lax.axis_index("head"), lax.axis_size("head")
    odd = ctx % 2
    first = 1 - odd
    is_last = (ctx == ctx_count - 1).astype(jnp.int32)
    spans = [ctx, 2 * ctx_count - 1 - ctx]
    span_first = jnp.where(first == 0, spans[0], spans[1])
    span_second = spans[0] + spans[1] - span_first
    place = jnp.stack([head, first, is_last, span_first, span_second]).astype(jnp.int32)
    block = shape((2, BLK, HD))
    partners = range(1, heads)
    swap = lambda x, t: lax.ppermute(x, "head", [(i, i ^ t) for i in range(heads)])
    outer = [p for i in range(1, ctx_count - 1, 2) for p in ((i, i + 1), (i + 1, i))]
    inner = [p for i in range(0, ctx_count, 2) for p in ((i, i + 1), (i + 1, i))]
    to_outer = lambda x: lax.ppermute(x, "ctx", outer)
    to_inner = lambda x: lax.ppermute(x, "ctx", inner)

    sends = call(functools.partial(pack_keys, heads), (place, key, value), [block] * (2 * (heads - 1)))
    received = [
        [swap(sends[half * (heads - 1) + t - 1], t) for t in partners] for half in range(2)
    ]
    joined = [
        call(
            functools.partial(join_keys, heads, half),
            (place, key, value, *received[half]),
            [shape((2, heads * BLK, HD)), shape((2, REACH * BLK, HD))],
        )
        for half in range(2)
    ]
    keys = [j[0] for j in joined]
    rim_second = to_outer(joined[0][1])
    rim_first = to_inner(joined[1][1])
    flops = 8 * BLK * BLK * HD * (query.shape[3] // HD) * REACH * (REACH + 1)

    def late(half):
        return call(
            functools.partial(late_blocks, heads, half),
            (place, doc_start, query, d_out, keys[half]),
            [shape(((heads - REACH) * BLK, query.shape[3])), shape((2, heads * BLK, HD), F32)],
            flops=flops,
            limit=20,
        )

    def early(half, incoming):
        return call(
            functools.partial(early_blocks, heads, half),
            (place, doc_start, query, d_out, keys[half], keys[1 - half], incoming),
            [
                shape((REACH * BLK, query.shape[3])),
                shape((2, REACH * BLK, HD), F32),
                shape((2, REACH * BLK, HD)),
            ],
            scratch=[
                pltpu.VMEM((2, 2 * REACH * BLK, HD), BF16),
                pltpu.VMEM((2, 2 * REACH * BLK, HD), F32),
            ],
            flops=flops,
            limit=20,
        )

    dq_late_first, late_first = late(0)
    dq_early_second, own_second, edge_second = early(1, rim_second)
    back_first = to_outer(edge_second)
    dq_early_first, own_first, edge_first = early(0, rim_first)
    back_second = to_inner(edge_first)
    dq_late_second, late_second = late(1)
    d_query = call(
        functools.partial(store_queries, REACH),
        (place, dq_early_first, dq_late_first, dq_early_second, dq_late_second),
        [shape(query.shape)],
        scratch=[pltpu.SemaphoreType.DMA((4,))],
        out_spec=pl.BlockSpec(memory_space=pl.ANY),
    )[0]

    def finish(half, d_late, d_own, d_back, d_local):
        parts = call(
            functools.partial(pack_grads, heads, half),
            (place, d_late, d_own, d_back, d_local),
            [block] * heads,
            scratch=[pltpu.VMEM((2, heads * BLK, HD), F32)],
        )
        return [parts[0]] + [swap(parts[t], t) for t in partners]

    parts_first = finish(0, late_first, own_first, back_first, edge_second)
    parts_second = finish(1, late_second, own_second, back_second, edge_first)
    d_key, d_value = call(
        functools.partial(join_grads, heads),
        (place, *parts_first, *parts_second),
        [shape(key.shape), shape(value.shape)],
    )
    return d_query, d_key, d_value


def solution(mesh):
    tokens = P("ctx", None, "head", None)
    columns = P("ctx", None, None, "head")
    return jax.shard_map(
        per_device,
        mesh=mesh,
        in_specs=(columns, tokens, tokens, columns, P()),
        out_specs=(columns, tokens, tokens),
        check_vma=False,
    )
```

```python
import functools

import jax
import jax.numpy as jnp
from jax import lax
from jax.experimental import pallas as pl
from jax.experimental.pallas import tpu as pltpu
from jax.sharding import PartitionSpec as P

HD = 128
BLK = 128
REACH = 2
SCALE = HD**-0.5
SCALE_LOG2E = SCALE * 1.4426950408889634
BF16 = jnp.bfloat16
F32 = jnp.float32
VMEM = pl.BlockSpec(memory_space=pltpu.VMEM)
HBM = pl.BlockSpec(memory_space=pltpu.HBM)
ANY = pl.BlockSpec(memory_space=pl.ANY)
SMEM = pl.BlockSpec(memory_space=pltpu.SMEM)


def shape(dims, dtype=BF16):
    return jax.ShapeDtypeStruct(dims, dtype)


def call(body, inputs, outs, scratch=(), flops=0, moved=0, limit=12, far=(), after=(), out_spec=VMEM):
    in_specs = [ANY] * len(after) + [
        SMEM if a.dtype == jnp.int32 else HBM if i in far else VMEM for i, a in enumerate(inputs)
    ]
    skip = len(after)
    name = body.func.__name__
    return pl.pallas_call(
        lambda *refs: body(*refs[skip:]),
        out_shape=outs,
        in_specs=in_specs,
        out_specs=[out_spec] * len(outs),
        scratch_shapes=list(scratch),
        compiler_params=pltpu.CompilerParams(vmem_limit_bytes=limit << 20),
        cost_estimate=pl.CostEstimate(flops=flops, bytes_accessed=moved, transcendentals=0),
        name=name,
    )(*after, *inputs)


def carry(pairs, sems):
    copies = [pltpu.make_async_copy(a, b, sems.at[i]) for i, (a, b) in enumerate(pairs)]
    for copy in copies:
        copy.start()
    for copy in copies:
        copy.wait()


def lanes(index):
    return pl.ds(pl.multiple_of(index * HD, HD), HD)


def rows(index, blocks=1):
    return pl.ds(pl.multiple_of(index * BLK, BLK), blocks * BLK)


def slot_of(place, half):
    return place[1] if half == 0 else 1 - place[1]


def pack_keys(heads, place, key, value, *refs):
    own, near, sends, sems = refs[0], refs[1], refs[2:-1], refs[-1]
    me = place[0]
    pairs = []
    for half in range(2):
        for t in range(heads):
            there = own.at[half] if t == 0 else near.at[half] if t == 1 else sends[half * (heads - 2) + t - 2]
            for i, array in enumerate((key, value)):
                pairs.append((array.at[0, slot_of(place, half), :, lanes(me ^ t)], there.at[i]))
    carry(pairs, sems)


def load_queries(doc_start, query, d_out, query_near, d_out_near, sems):
    carry([(query, query_near), (d_out, d_out_near)], sems)


def join_keys(heads, half, place, own, near, *refs):
    parts, (span, rim) = refs[: heads - 2], refs[heads - 2 :]
    me = place[0]
    for t in range(heads):
        part = own.at[half] if t == 0 else near.at[half] if t == 1 else parts[t - 2]
        span[0, rows(me ^ t), :] = part[0]
        span[1, rows(me ^ t), :] = part[1]
    rim[...] = span[:, (heads - REACH) * BLK :, :]


def dot(a, b, ca, cb):
    return lax.dot_general(a, b, (((ca,), (cb,)), ((), ())), preferred_element_type=F32)


def block_grads(n, first, queries, grads, keys, d_queries, d_keys):
    count = queries.shape[1] // HD
    window = pl.ds(first * BLK, n * BLK)
    k, v = keys[0, window, :], keys[1, window, :]
    q = jnp.concatenate([queries[:, j * HD : (j + 1) * HD] for j in range(count)], axis=0)
    do = jnp.concatenate([grads[:, j * HD : (j + 1) * HD] for j in range(count)], axis=0)
    s = dot(k, q, 1, 1)
    dp = dot(v, do, 1, 1)
    token = lax.broadcasted_iota(jnp.int32, (BLK, count * BLK), 1) & (BLK - 1)
    seen = lax.broadcasted_iota(jnp.int32, (BLK, count * BLK), 0) <= token
    last = jnp.where(seen, s[(n - 1) * BLK :], -jnp.inf)
    s = jnp.concatenate([s[: (n - 1) * BLK], last], axis=0) if n > 1 else last
    peak = jnp.max(s, axis=0, keepdims=True)
    w = jnp.exp2((s - peak) * SCALE_LOG2E)
    inverse = 1.0 / jnp.sum(w, axis=0, keepdims=True)
    delta = jnp.sum(w * dp, axis=0, keepdims=True) * inverse
    p = w * inverse
    ds = (p * (dp - delta)).astype(BF16)
    d_keys[0, window, :] += dot(ds, q, 1, 0) * SCALE
    d_keys[1, window, :] += dot(p.astype(BF16), do, 1, 0)
    dq = (dot(k.T, ds, 1, 0) * SCALE).astype(BF16)
    for j in range(count):
        d_queries[:, j * HD : (j + 1) * HD] = dq[:, j * BLK : (j + 1) * BLK].T


def span_part(first_block, blocks, per_span, half, place, doc_start, query, d_out, keys, d_query, d_keys):
    slot = slot_of(place, half)
    d_keys[...] = jnp.zeros_like(d_keys)
    for b in range(blocks):
        block = place[3 + slot] * per_span + first_block + b
        before = doc_start[jnp.maximum(block - 1, 0)]
        visible = jnp.where(doc_start[block] == 1, 1, jnp.where(before == 1, 2, 3))
        tokens = pl.ds((first_block + b) * BLK, BLK)
        for n in range(1, REACH + 2):

            @pl.when(visible == n)
            def _(n=n, tokens=tokens, b=b):
                block_grads(
                    n,
                    b + REACH + 1 - n,
                    query.at[0, slot, tokens, :],
                    d_out.at[0, slot, tokens, :],
                    keys,
                    d_query.at[pl.ds(b * BLK, BLK), :],
                    d_keys,
                )


def late_blocks(per_span, half, place, doc_start, query, d_out, keys, d_query, d_keys):
    span_part(REACH, per_span - REACH, per_span, half, place, doc_start, query, d_out, keys, d_query, d_keys)


def early_blocks(per_span, half, place, doc_start, query, d_out, keys, other, incoming, d_query, d_own, d_rim, window, d_window):
    cut = REACH * BLK
    window[:, cut:, :] = keys[:, :cut, :]
    window[:, :cut, :] = incoming[...]
    if half == 1:

        @pl.when(place[2] == 1)
        def _():
            window[:, :cut, :] = other[:, (per_span - REACH) * BLK :, :]

    span_part(0, REACH, per_span, half, place, doc_start, query, d_out, window, d_query, d_window)
    d_rim[...] = d_window[:, :cut, :].astype(BF16)
    d_own[...] = d_window[:, cut:, :]


def store_queries(reach, place, early_first, late_first, early_second, late_second, d_query, sems):
    pairs = []
    for half, parts in ((0, (early_first, late_first)), (1, (early_second, late_second))):
        for part, start in zip(parts, (0, reach * BLK)):
            pairs.append((part, d_query.at[0, slot_of(place, half), pl.ds(start, part.shape[0]), :]))
    carry(pairs, sems)


def pack_grads(heads, place, late_0, own_0, back_0, edge_0, late_1, own_1, back_1, edge_1, *refs):
    sends, total = refs[:-1], refs[-1]
    me = place[0]
    cut = REACH * BLK
    for half, (late, own, back) in enumerate(((late_0, own_0, back_0), (late_1, own_1, back_1))):
        total[...] = late[...]
        total[:, :cut, :] += own[...]
        total[:, (heads - REACH) * BLK :, :] += back[...].astype(F32)
        if half == 0:

            @pl.when(place[2] == 1)
            def _():
                total[:, (heads - REACH) * BLK :, :] += edge_1[...].astype(F32)

        for t in range(heads):
            sends[t][half] = total[:, rows(me ^ t), :].astype(BF16)


def join_grads(heads, place, *refs):
    parts, (d_key, d_value, sems) = refs[:heads], refs[heads:]
    me = place[0]
    pairs = []
    for t in range(heads):
        for half in range(2):
            for i, array in enumerate((d_key, d_value)):
                pairs.append(
                    (parts[t].at[half, i], array.at[0, slot_of(place, half), :, lanes(me ^ t)])
                )
    carry(pairs, sems)


def per_device(query, key, value, d_out, doc_start):
    ctx, ctx_count = lax.axis_index("ctx"), lax.axis_size("ctx")
    head, heads = lax.axis_index("head"), lax.axis_size("head")
    odd = ctx % 2
    first = 1 - odd
    is_last = (ctx == ctx_count - 1).astype(jnp.int32)
    place = jnp.stack([head, first, is_last, ctx, 2 * ctx_count - 1 - ctx]).astype(jnp.int32)
    block = shape((2, BLK, HD))
    partners = range(1, heads)
    swap = lambda x, t: lax.ppermute(x, "head", [(i, i ^ t) for i in range(heads)])
    outer = [p for i in range(1, ctx_count - 1, 2) for p in ((i, i + 1), (i + 1, i))]
    inner = [p for i in range(0, ctx_count, 2) for p in ((i, i + 1), (i + 1, i))]
    to_outer = lambda x: lax.ppermute(x, "ctx", outer)
    to_inner = lambda x: lax.ppermute(x, "ctx", inner)

    key, value, query, d_out = (
        pltpu.with_memory_space_constraint(x, pltpu.HBM) for x in (key, value, query, d_out)
    )
    own, near, *sends = call(
        functools.partial(pack_keys, heads),
        (place, key, value),
        [shape((2, 2, BLK, HD))] * 2 + [block] * (2 * (heads - 2)),
        scratch=[pltpu.SemaphoreType.DMA((4 * heads,))],
        far=(1, 2),
    )
    near = swap(near, 1)
    parts = [
        [swap(sends[half * (heads - 2) + t - 2], t) for t in range(2, heads)] for half in range(2)
    ]
    query, d_out = call(
        functools.partial(load_queries),
        (doc_start, query, d_out),
        [shape(query.shape), shape(d_out.shape)],
        scratch=[pltpu.SemaphoreType.DMA((2,))],
        moved=4 * query.size,
        far=(1, 2),
        after=(own,),
    )
    joined = []
    for half in range(2):
        joined.append(
            call(
                functools.partial(join_keys, heads, half),
                (place, own, near, *parts[half]),
                [shape((2, heads * BLK, HD)), shape((2, REACH * BLK, HD))],
                after=(query,) if half == 0 else (joined[0][1],),
            )
        )
    keys = [j[0] for j in joined]
    rim_second = to_outer(joined[0][1])
    rim_first = to_inner(joined[1][1])
    flops = 8 * BLK * BLK * HD * (query.shape[3] // HD) * REACH * (REACH + 1)

    def late(half, after):
        return call(
            functools.partial(late_blocks, heads, half),
            (place, doc_start, query, d_out, keys[half]),
            [shape(((heads - REACH) * BLK, query.shape[3])), shape((2, heads * BLK, HD), F32)],
            flops=flops,
            limit=20,
            after=after,
        )

    def early(half, incoming, after):
        return call(
            functools.partial(early_blocks, heads, half),
            (place, doc_start, query, d_out, keys[half], keys[1 - half], incoming),
            [
                shape((REACH * BLK, query.shape[3])),
                shape((2, REACH * BLK, HD), F32),
                shape((2, REACH * BLK, HD)),
            ],
            scratch=[
                pltpu.VMEM((2, 2 * REACH * BLK, HD), BF16),
                pltpu.VMEM((2, 2 * REACH * BLK, HD), F32),
            ],
            flops=flops,
            limit=20,
            after=after,
        )

    dq_late_first, late_first = late(0, (joined[1][1],))
    dq_early_second, own_second, edge_second = early(1, rim_second, (late_first,))
    back_first = to_outer(edge_second)
    dq_early_first, own_first, edge_first = early(0, rim_first, (edge_second,))
    back_second = to_inner(edge_first)
    dq_late_second, late_second = late(1, (edge_first,))
    d_query = call(
        functools.partial(store_queries, REACH),
        (place, dq_early_first, dq_late_first, dq_early_second, dq_late_second),
        [shape(query.shape)],
        scratch=[pltpu.SemaphoreType.DMA((4,))],
        out_spec=ANY,
    )[0]

    grads = call(
        functools.partial(pack_grads, heads),
        (place, late_first, own_first, back_first, edge_first)
        + (late_second, own_second, back_second, edge_second),
        [shape((2, 2, BLK, HD))] * heads,
        scratch=[pltpu.VMEM((2, heads * BLK, HD), F32)],
    )
    d_key, d_value = call(
        functools.partial(join_grads, heads),
        (place, grads[0], *[swap(grads[t], t) for t in partners]),
        [shape(key.shape), shape(value.shape)],
        scratch=[pltpu.SemaphoreType.DMA((4 * heads,))],
        out_spec=ANY,
    )
    return d_query, d_key, d_value


def solution(mesh):
    tokens = P("ctx", None, "head", None)
    columns = P("ctx", None, None, "head")
    return jax.shard_map(
        per_device,
        mesh=mesh,
        in_specs=(columns, tokens, tokens, columns, P()),
        out_specs=(columns, tokens, tokens),
        check_vma=False,
    )
```

```python
import functools

import jax
import jax.numpy as jnp
from jax import lax
from jax.experimental import pallas as pl
from jax.experimental.pallas import tpu as pltpu
from jax.sharding import PartitionSpec as P

HD = 128
BLK = 128
REACH = 2
SCALE = HD**-0.5
SCALE_LOG2E = SCALE * 1.4426950408889634
BF16 = jnp.bfloat16
F32 = jnp.float32
VMEM = pl.BlockSpec(memory_space=pltpu.VMEM)
HBM = pl.BlockSpec(memory_space=pltpu.HBM)
ANY = pl.BlockSpec(memory_space=pl.ANY)


def shape(dims, dtype=BF16):
    return jax.ShapeDtypeStruct(dims, dtype)


def call(body, inputs, outs, scratch=(), flops=0, moved=0, limit=12, far=(), after=(), out_spec=VMEM, aliases=None):
    in_specs = [ANY] * len(after) + [
        HBM if i in far else VMEM for i in range(len(inputs))
    ]
    skip = len(after)
    name = body.func.__name__
    return pl.pallas_call(
        lambda *refs: body(*refs[skip:]),
        out_shape=outs,
        in_specs=in_specs,
        out_specs=[out_spec] * len(outs),
        scratch_shapes=list(scratch),
        input_output_aliases=aliases or {},
        compiler_params=pltpu.CompilerParams(vmem_limit_bytes=limit << 20),
        cost_estimate=pl.CostEstimate(flops=flops, bytes_accessed=moved, transcendentals=0),
        name=name,
    )(*after, *inputs)


def carry(pairs, sems):
    copies = [pltpu.make_async_copy(a, b, sems.at[i]) for i, (a, b) in enumerate(pairs)]
    for copy in copies:
        copy.start()
    for copy in copies:
        copy.wait()


def lanes(index):
    return pl.ds(pl.multiple_of(index * HD, HD), HD)


def rows(index, blocks=1):
    return pl.ds(pl.multiple_of(index * BLK, BLK), blocks * BLK)


def slot_of(half):
    odd = lax.rem(lax.axis_index("ctx"), 2)
    return 1 - odd if half == 0 else odd


def is_last():
    return lax.axis_index("ctx") == lax.axis_size("ctx") - 1


def span_of(half):
    ctx = lax.axis_index("ctx")
    return jnp.where(slot_of(half) == 0, ctx, 2 * lax.axis_size("ctx") - 1 - ctx)


def pack_keys(heads, key, value, *refs):
    own, near, sends, sems = refs[0], refs[1], refs[2:-1], refs[-1]
    me = lax.axis_index("head")
    pairs = []
    for half in range(2):
        for t in range(heads):
            there = own.at[half] if t == 0 else near.at[half] if t == 1 else sends[half * (heads - 2) + t - 2]
            for i, array in enumerate((key, value)):
                pairs.append((array.at[0, slot_of(half), :, lanes(me ^ t)], there.at[i]))
    carry(pairs, sems)


def load_queries(doc_start, query, d_out, starts_near, query_near, d_out_near, sems):
    carry([(doc_start, starts_near), (query, query_near), (d_out, d_out_near)], sems)


def join_keys(heads, half, own, near, *refs):
    parts, (span, rim) = refs[: heads - 2], refs[heads - 2 :]
    me = lax.axis_index("head")
    for t in range(heads):
        part = own.at[half] if t == 0 else near.at[half] if t == 1 else parts[t - 2]
        span[0, rows(me ^ t), :] = part[0]
        span[1, rows(me ^ t), :] = part[1]
    rim[...] = span[:, (heads - REACH) * BLK :, :]


def dot(a, b, ca, cb):
    return lax.dot_general(a, b, (((ca,), (cb,)), ((), ())), preferred_element_type=F32)


def block_grads(n, first, queries, grads, keys, d_queries, d_keys):
    count = queries.shape[1] // HD
    window = pl.ds(first * BLK, n * BLK)
    k, v = keys[0, window, :], keys[1, window, :]
    q = jnp.concatenate([queries[:, j * HD : (j + 1) * HD] for j in range(count)], axis=0)
    do = jnp.concatenate([grads[:, j * HD : (j + 1) * HD] for j in range(count)], axis=0)
    s = dot(k, q, 1, 1)
    dp = dot(v, do, 1, 1)
    token = lax.broadcasted_iota(jnp.int32, (BLK, count * BLK), 1) & (BLK - 1)
    seen = lax.broadcasted_iota(jnp.int32, (BLK, count * BLK), 0) <= token
    last = jnp.where(seen, s[(n - 1) * BLK :], -jnp.inf)
    s = jnp.concatenate([s[: (n - 1) * BLK], last], axis=0) if n > 1 else last
    peak = jnp.max(s, axis=0, keepdims=True)
    w = jnp.exp2((s - peak) * SCALE_LOG2E)
    inverse = 1.0 / jnp.sum(w, axis=0, keepdims=True)
    delta = jnp.sum(w * dp, axis=0, keepdims=True) * inverse
    p = w * inverse
    ds = (p * (dp - delta)).astype(BF16)
    d_keys[0, window, :] += dot(ds, q, 1, 0) * SCALE
    d_keys[1, window, :] += dot(p.astype(BF16), do, 1, 0)
    dq = (dot(k.T, ds, 1, 0) * SCALE).astype(BF16)
    for j in range(count):
        d_queries[:, j * HD : (j + 1) * HD] = dq[:, j * BLK : (j + 1) * BLK].T


def span_part(first_block, blocks, per_span, half, doc_start, query, d_out, keys, d_query, d_keys):
    slot = slot_of(half)
    d_keys[...] = jnp.zeros_like(d_keys)
    for b in range(blocks):
        block = span_of(half) * per_span + first_block + b
        spot = lax.broadcasted_iota(jnp.int32, doc_start.shape, 1)
        marks = doc_start[...].astype(F32)
        mark = jnp.sum(jnp.where(spot == block, 2 * marks, jnp.where(spot == block - 1, marks, 0.0)))
        visible = jnp.where(mark > 1.5, 1, jnp.where(mark > 0.5, 2, 3))
        tokens = pl.ds((first_block + b) * BLK, BLK)
        for n in range(1, REACH + 2):

            @pl.when(visible == n)
            def _(n=n, tokens=tokens, b=b):
                block_grads(
                    n,
                    b + REACH + 1 - n,
                    query.at[0, slot, tokens, :],
                    d_out.at[0, slot, tokens, :],
                    keys,
                    d_query.at[pl.ds(b * BLK, BLK), :],
                    d_keys,
                )


def late_blocks(per_span, half, doc_start, query, d_out, keys, d_query, d_keys):
    span_part(REACH, per_span - REACH, per_span, half, doc_start, query, d_out, keys, d_query, d_keys)


def early_blocks(per_span, half, doc_start, query, d_out, keys, other, incoming, d_query, d_own, d_rim, window, d_window):
    cut = REACH * BLK
    window[:, cut:, :] = keys[:, :cut, :]
    window[:, :cut, :] = incoming[...]
    if half == 1:

        @pl.when(is_last())
        def _():
            window[:, :cut, :] = other[:, (per_span - REACH) * BLK :, :]

    span_part(0, REACH, per_span, half, doc_start, query, d_out, window, d_query, d_window)
    d_rim[...] = d_window[:, :cut, :].astype(BF16)
    d_own[...] = d_window[:, cut:, :]


def store_queries(reach, early_first, late_first, early_second, late_second, d_query, sems):
    pairs = []
    for half, parts in ((0, (early_first, late_first)), (1, (early_second, late_second))):
        for part, start in zip(parts, (0, reach * BLK)):
            pairs.append((part, d_query.at[0, slot_of(half), pl.ds(start, part.shape[0]), :]))
    carry(pairs, sems)


def pack_grads(heads, half, late, own, back, local, *refs):
    sends, total = refs[:-1], refs[-1]
    me = lax.axis_index("head")
    cut = REACH * BLK
    total[...] = late[...]
    total[:, :cut, :] += own[...]
    total[:, (heads - REACH) * BLK :, :] += back[...].astype(F32)
    if half == 0:

        @pl.when(is_last())
        def _():
            total[:, (heads - REACH) * BLK :, :] += local[...].astype(F32)

    for t in range(heads):
        sends[t][...] = total[:, rows(me ^ t), :].astype(BF16)


def join_grads(heads, half, *refs):
    parts, (d_key, d_value, sems) = refs[:heads], refs[-3:]
    me = lax.axis_index("head")
    pairs = []
    for t in range(heads):
        for i, array in enumerate((d_key, d_value)):
            pairs.append((parts[t].at[i], array.at[0, slot_of(half), :, lanes(me ^ t)]))
    carry(pairs, sems)


def per_device(query, key, value, d_out, doc_start):
    ctx_count, heads = lax.axis_size("ctx"), lax.axis_size("head")
    block = shape((2, BLK, HD))
    partners = range(1, heads)
    swap = lambda x, t: lax.ppermute(x, "head", [(i, i ^ t) for i in range(heads)])
    outer = [p for i in range(1, ctx_count - 1, 2) for p in ((i, i + 1), (i + 1, i))]
    inner = [p for i in range(0, ctx_count, 2) for p in ((i, i + 1), (i + 1, i))]
    to_outer = lambda x: lax.ppermute(x, "ctx", outer)
    to_inner = lambda x: lax.ppermute(x, "ctx", inner)

    key, value, query, d_out = (
        pltpu.with_memory_space_constraint(x, pltpu.HBM) for x in (key, value, query, d_out)
    )
    own, near, *sends = call(
        functools.partial(pack_keys, heads),
        (key, value),
        [shape((2, 2, BLK, HD))] * 2 + [block] * (2 * (heads - 2)),
        scratch=[pltpu.SemaphoreType.DMA((4 * heads,))],
        far=(0, 1),
    )
    near = swap(near, 1)
    parts = [
        [swap(sends[half * (heads - 2) + t - 2], t) for t in range(2, heads)] for half in range(2)
    ]
    starts = pltpu.with_memory_space_constraint(doc_start[None], pltpu.HBM)
    starts, query, d_out = call(
        functools.partial(load_queries),
        (starts, query, d_out),
        [shape(starts.shape, jnp.int32), shape(query.shape), shape(d_out.shape)],
        scratch=[pltpu.SemaphoreType.DMA((3,))],
        moved=4 * query.size,
        far=(0, 1, 2),
        after=(own,),
    )
    joined = []
    for half in range(2):
        joined.append(
            call(
                functools.partial(join_keys, heads, half),
                (own, near, *parts[half]),
                [shape((2, heads * BLK, HD)), shape((2, REACH * BLK, HD))],
                after=(query,) if half == 0 else (joined[0][1],),
            )
        )
    keys = [j[0] for j in joined]
    rim_second = to_outer(joined[0][1])
    rim_first = to_inner(joined[1][1])

    def late(half, after):
        return call(
            functools.partial(late_blocks, heads, half),
            (starts, query, d_out, keys[half]),
            [shape(((heads - REACH) * BLK, query.shape[3])), shape((2, heads * BLK, HD), F32)],
            limit=20,
            after=after,
        )

    def early(half, incoming, after):
        return call(
            functools.partial(early_blocks, heads, half),
            (starts, query, d_out, keys[half], keys[1 - half], incoming),
            [
                shape((REACH * BLK, query.shape[3])),
                shape((2, REACH * BLK, HD), F32),
                shape((2, REACH * BLK, HD)),
            ],
            scratch=[
                pltpu.VMEM((2, 2 * REACH * BLK, HD), BF16),
                pltpu.VMEM((2, 2 * REACH * BLK, HD), F32),
            ],
            limit=20,
            after=after,
        )

    dq_late_first, late_first = late(0, (joined[1][1],))
    dq_late_second, late_second = late(1, (late_first,))
    dq_early_second, own_second, edge_second = early(1, rim_second, (late_second,))
    back_first = to_outer(edge_second)
    dq_early_first, own_first, edge_first = early(0, rim_first, (edge_second,))
    back_second = to_inner(edge_first)
    d_query = call(
        functools.partial(store_queries, REACH),
        (dq_early_first, dq_late_first, dq_early_second, dq_late_second),
        [shape(query.shape)],
        scratch=[pltpu.SemaphoreType.DMA((4,))],
        out_spec=ANY,
    )[0]

    d_keys, packed = (), ()
    for half, late_part, own_part, back, local in (
        (0, late_first, own_first, back_first, edge_second),
        (1, late_second, own_second, back_second, edge_first),
    ):
        packed = call(
            functools.partial(pack_grads, heads, half),
            (late_part, own_part, back, local),
            [block] * heads,
            scratch=[pltpu.VMEM((2, heads * BLK, HD), F32)],
            after=packed[:1],
        )
        inputs = (packed[0], *[swap(packed[t], t) for t in partners], *d_keys)
        d_keys = call(
            functools.partial(join_grads, heads, half),
            inputs,
            [shape(key.shape), shape(value.shape)],
            scratch=[pltpu.SemaphoreType.DMA((2 * heads,))],
            far=range(heads, len(inputs)),
            out_spec=HBM,
            aliases={heads + i: i for i in range(len(d_keys))},
        )
    d_key, d_value = d_keys
    return d_query, d_key, d_value


def solution(mesh):
    tokens = P("ctx", None, "head", None)
    columns = P("ctx", None, None, "head")
    return jax.shard_map(
        per_device,
        mesh=mesh,
        in_specs=(columns, tokens, tokens, columns, P()),
        out_specs=(columns, tokens, tokens),
        check_vma=False,
    )
```

```python
import functools

import jax
import jax.numpy as jnp
from jax import lax
from jax.experimental import pallas as pl
from jax.experimental.pallas import tpu as pltpu
from jax.sharding import PartitionSpec as P

HD = 128
BLK = 128
REACH = 2
SCALE = HD**-0.5
SCALE_LOG2E = SCALE * 1.4426950408889634
LATE = ((1, 1), (1, 2), (2, 1), (3, 1))
EARLY = ((2, 3), (3, 1))
BF16 = jnp.bfloat16
F32 = jnp.float32
VMEM = pl.BlockSpec(memory_space=pltpu.VMEM)
HBM = pl.BlockSpec(memory_space=pltpu.HBM)
ANY = pl.BlockSpec(memory_space=pl.ANY)


def shape(dims, dtype=BF16):
    return jax.ShapeDtypeStruct(dims, dtype)


def call(body, inputs, outs, scratch=(), flops=0, moved=0, limit=12, far=(), after=(), out_spec=VMEM, aliases=None):
    in_specs = [ANY] * len(after) + [
        HBM if i in far else VMEM for i in range(len(inputs))
    ]
    skip = len(after)
    name = body.func.__name__
    return pl.pallas_call(
        lambda *refs: body(*refs[skip:]),
        out_shape=outs,
        in_specs=in_specs,
        out_specs=[out_spec] * len(outs),
        scratch_shapes=list(scratch),
        input_output_aliases=aliases or {},
        compiler_params=pltpu.CompilerParams(vmem_limit_bytes=limit << 20),
        cost_estimate=pl.CostEstimate(flops=flops, bytes_accessed=moved, transcendentals=0),
        name=name,
    )(*after, *inputs)


def carry(pairs, sems):
    copies = [pltpu.make_async_copy(a, b, sems.at[i]) for i, (a, b) in enumerate(pairs)]
    for copy in copies:
        copy.start()
    for copy in copies:
        copy.wait()


def lanes(index):
    return pl.ds(pl.multiple_of(index * HD, HD), HD)


def rows(index, blocks=1):
    return pl.ds(pl.multiple_of(index * BLK, BLK), blocks * BLK)


def slot_of(half):
    odd = lax.rem(lax.axis_index("ctx"), 2)
    return 1 - odd if half == 0 else odd


def is_last():
    return lax.axis_index("ctx") == lax.axis_size("ctx") - 1


def span_of(half):
    ctx = lax.axis_index("ctx")
    return jnp.where(slot_of(half) == 0, ctx, 2 * lax.axis_size("ctx") - 1 - ctx)


def pack_keys(heads, key, value, *refs):
    own, near, sends, sems = refs[0], refs[1], refs[2:-1], refs[-1]
    me = lax.axis_index("head")
    pairs = []
    for half in range(2):
        for t in range(heads):
            there = own.at[half] if t == 0 else near.at[half] if t == 1 else sends[half * (heads - 2) + t - 2]
            for i, array in enumerate((key, value)):
                pairs.append((array.at[0, slot_of(half), :, lanes(me ^ t)], there.at[i]))
    carry(pairs, sems)


def load_queries(doc_start, query, d_out, starts_near, query_near, d_out_near, sems):
    carry([(doc_start, starts_near), (query, query_near), (d_out, d_out_near)], sems)


def join_keys(heads, half, own, near, *refs):
    parts, (span, rim) = refs[: heads - 2], refs[heads - 2 :]
    me = lax.axis_index("head")
    for t in range(heads):
        part = own.at[half] if t == 0 else near.at[half] if t == 1 else parts[t - 2]
        span[0, rows(me ^ t), :] = part[0]
        span[1, rows(me ^ t), :] = part[1]
    rim[...] = span[:, (heads - REACH) * BLK :, :]


def dot(a, b, ca, cb):
    return lax.dot_general(a, b, (((ca,), (cb,)), ((), ())), preferred_element_type=F32)


def products(task):
    n, first, queries, grads, keys, d_queries = task
    count = queries.shape[1] // HD
    window = pl.ds(first * BLK, n * BLK)
    k, v = keys[0, window, :], keys[1, window, :]
    q = jnp.concatenate([queries[:, j * HD : (j + 1) * HD] for j in range(count)], axis=0)
    do = jnp.concatenate([grads[:, j * HD : (j + 1) * HD] for j in range(count)], axis=0)
    return k, q, do, dot(k, q, 1, 1), dot(v, do, 1, 1)


def weigh(task, k, q, do, s, dp):
    n = task[0]
    seen = lax.broadcasted_iota(jnp.int32, (BLK, BLK), 0) <= lax.broadcasted_iota(jnp.int32, (BLK, BLK), 1)
    hide = jnp.where(seen, 0.0, -jnp.inf)
    ps, dss = [], []
    for j in range(s.shape[1] // BLK):
        p_, ds_ = weigh_head(n, hide, s[:, j * BLK : (j + 1) * BLK], dp[:, j * BLK : (j + 1) * BLK])
        ps.append(p_)
        dss.append(ds_)
    return k, q, do, jnp.concatenate(ps, axis=1), jnp.concatenate(dss, axis=1)


def weigh_head(n, hide, s, dp):
    last = s[(n - 1) * BLK :] + hide
    return weigh_all(jnp.concatenate([s[: (n - 1) * BLK], last], axis=0) if n > 1 else last, dp)


def weigh_all(s, dp):
    peak = jnp.max(s, axis=0, keepdims=True)
    w = jnp.exp2((s - peak) * SCALE_LOG2E)
    inverse = 1.0 / jnp.sum(w, axis=0, keepdims=True)
    delta = jnp.sum(w * dp, axis=0, keepdims=True) * inverse
    p = w * inverse
    return p.astype(BF16), (p * (dp - delta)).astype(BF16)


def gather(task, d_keys, k, q, do, p, ds):
    n, first, queries, grads, keys, d_queries = task
    window = pl.ds(first * BLK, n * BLK)
    d_keys[0, window, :] += dot(ds, q, 1, 0) * SCALE
    d_keys[1, window, :] += dot(p, do, 1, 0)
    dq = (dot(k.T, ds, 1, 0) * SCALE).astype(BF16)
    for j in range(dq.shape[1] // BLK):
        d_queries[:, j * HD : (j + 1) * HD] = dq[:, j * BLK : (j + 1) * BLK].T


def pair_grads(a, b, d_keys):
    pa = products(a)
    wa = weigh(a, *pa)
    pb = products(b)
    gather(a, d_keys, *wa)
    wb = weigh(b, *pb)
    gather(b, d_keys, *wb)


def loose_grads(reach, first_block, slot, visible, query, d_out, keys, d_query, d_keys):
    group = 4
    steps = query.shape[3] // (group * HD)
    seen_rows = (reach + 1) * BLK

    def step(i, carried):
        b, g = i // steps, lax.rem(i, steps)
        tokens = rows(first_block + b)
        window = rows(b + REACH - reach, reach + 1)
        columns = [lanes(g * group + j) for j in range(group)]
        q = jnp.concatenate([query[0, slot, tokens, c] for c in columns], axis=0)
        do = jnp.concatenate([d_out[0, slot, tokens, c] for c in columns], axis=0)
        k, v = keys[0, window, :], keys[1, window, :]
        count = jnp.where(b == 0, visible[0], visible[1])
        place = lax.broadcasted_iota(jnp.int32, (seen_rows, BLK), 0)
        token = lax.broadcasted_iota(jnp.int32, (seen_rows, BLK), 1)
        seen = (place >= (reach + 1 - count) * BLK) & (place - reach * BLK <= token)
        hide = jnp.where(seen, 0.0, -jnp.inf)
        s, dp = dot(k, q, 1, 1), dot(v, do, 1, 1)
        p, ds = weigh_all(s + jnp.concatenate([hide] * group, axis=1), dp)
        d_keys[0, window, :] += dot(ds, q, 1, 0) * SCALE
        d_keys[1, window, :] += dot(p, do, 1, 0)
        dq = (dot(k.T, ds, 1, 0) * SCALE).astype(BF16)
        for j, c in enumerate(columns):
            d_query[rows(b), c] = dq[:, j * BLK : (j + 1) * BLK].T
        return carried

    lax.fori_loop(0, 2 * steps, step, 0)


def span_part(fast, reach, first_block, per_span, half, doc_start, query, d_out, keys, d_query, d_keys):
    slot = slot_of(half)
    d_keys[...] = jnp.zeros_like(d_keys)
    spot = lax.broadcasted_iota(jnp.int32, doc_start.shape, 1)
    marks = doc_start[...].astype(F32)
    visible = []
    for b in range(2):
        block = span_of(half) * per_span + first_block + b
        mark = jnp.sum(jnp.where(spot == block, 2 * marks, jnp.where(spot == block - 1, marks, 0.0)))
        visible.append(jnp.where(mark > 1.5, 1, jnp.where(mark > 0.5, 2, 3)))

    def task(b, n):
        tokens = pl.ds((first_block + b) * BLK, BLK)
        return (
            n,
            b + REACH + 1 - n,
            query.at[0, slot, tokens, :],
            d_out.at[0, slot, tokens, :],
            keys,
            d_query.at[pl.ds(b * BLK, BLK), :],
        )

    common = [(n, then) for n in range(1, REACH + 2) for then in (1, n + 1) if then <= REACH + 1]
    common = [case for case in common if case in fast]
    chosen = False
    for n, then in common:
        here = (visible[0] == n) & (visible[1] == then)
        chosen = here | chosen

        @pl.when(here)
        def _(n=n, then=then):
            pair_grads(task(0, n), task(1, then), d_keys)

    @pl.when(jnp.logical_not(chosen))
    def _():
        loose_grads(reach, first_block, slot, visible, query, d_out, keys, d_query, d_keys)


def late_blocks(per_span, half, doc_start, query, d_out, keys, d_query, d_keys):
    span_part(LATE, REACH, REACH, per_span, half, doc_start, query, d_out, keys, d_query, d_keys)


def early_blocks(per_span, half, doc_start, query, d_out, keys, other, incoming, d_query, d_own, d_rim, window, d_window):
    cut = REACH * BLK
    window[:, cut:, :] = keys[:, :cut, :]
    window[:, :cut, :] = incoming[...]
    if half == 1:

        @pl.when(is_last())
        def _():
            window[:, :cut, :] = other[:, (per_span - REACH) * BLK :, :]

    span_part(EARLY, REACH - 1, 0, per_span, half, doc_start, query, d_out, window, d_query, d_window)
    d_rim[...] = d_window[:, :cut, :].astype(BF16)
    d_own[...] = d_window[:, cut:, :]


def store_queries(reach, early_first, late_first, early_second, late_second, d_query, sems):
    pairs = []
    for half, parts in ((0, (early_first, late_first)), (1, (early_second, late_second))):
        for part, start in zip(parts, (0, reach * BLK)):
            pairs.append((part, d_query.at[0, slot_of(half), pl.ds(start, part.shape[0]), :]))
    carry(pairs, sems)


def pack_grads(heads, half, late, own, back, local, *refs):
    sends, total = refs[:-1], refs[-1]
    me = lax.axis_index("head")
    cut = REACH * BLK
    total[...] = late[...]
    total[:, :cut, :] += own[...]
    total[:, (heads - REACH) * BLK :, :] += back[...].astype(F32)
    if half == 0:

        @pl.when(is_last())
        def _():
            total[:, (heads - REACH) * BLK :, :] += local[...].astype(F32)

    for t in range(heads):
        sends[t][...] = total[:, rows(me ^ t), :].astype(BF16)


def join_grads(heads, half, *refs):
    parts, (d_key, d_value, sems) = refs[:heads], refs[-3:]
    me = lax.axis_index("head")
    pairs = []
    for t in range(heads):
        for i, array in enumerate((d_key, d_value)):
            pairs.append((parts[t].at[i], array.at[0, slot_of(half), :, lanes(me ^ t)]))
    carry(pairs, sems)


def per_device(query, key, value, d_out, doc_start):
    ctx_count, heads = lax.axis_size("ctx"), lax.axis_size("head")
    block = shape((2, BLK, HD))
    partners = range(1, heads)
    swap = lambda x, t: lax.ppermute(x, "head", [(i, i ^ t) for i in range(heads)])
    outer = [p for i in range(1, ctx_count - 1, 2) for p in ((i, i + 1), (i + 1, i))]
    inner = [p for i in range(0, ctx_count, 2) for p in ((i, i + 1), (i + 1, i))]
    to_outer = lambda x: lax.ppermute(x, "ctx", outer)
    to_inner = lambda x: lax.ppermute(x, "ctx", inner)

    key, value, query, d_out = (
        pltpu.with_memory_space_constraint(x, pltpu.HBM) for x in (key, value, query, d_out)
    )
    own, near, *sends = call(
        functools.partial(pack_keys, heads),
        (key, value),
        [shape((2, 2, BLK, HD))] * 2 + [block] * (2 * (heads - 2)),
        scratch=[pltpu.SemaphoreType.DMA((4 * heads,))],
        far=(0, 1),
    )
    near = swap(near, 1)
    parts = [
        [swap(sends[half * (heads - 2) + t - 2], t) for t in range(2, heads)] for half in range(2)
    ]
    starts = pltpu.with_memory_space_constraint(doc_start[None], pltpu.HBM)
    starts, query, d_out = call(
        functools.partial(load_queries),
        (starts, query, d_out),
        [shape(starts.shape, jnp.int32), shape(query.shape), shape(d_out.shape)],
        scratch=[pltpu.SemaphoreType.DMA((3,))],
        moved=4 * query.size,
        far=(0, 1, 2),
        after=(own,),
    )
    def join(half, after):
        return call(
            functools.partial(join_keys, heads, half),
            (own, near, *parts[half]),
            [shape((2, heads * BLK, HD)), shape((2, REACH * BLK, HD))],
            after=after,
        )

    keys = [None, None]
    keys[0], rim = join(0, (query,))
    rim_second = to_outer(rim)

    def late(half, after):
        return call(
            functools.partial(late_blocks, heads, half),
            (starts, query, d_out, keys[half]),
            [shape(((heads - REACH) * BLK, query.shape[3])), shape((2, heads * BLK, HD), F32)],
            limit=20,
            after=after,
        )

    def early(half, incoming, after):
        return call(
            functools.partial(early_blocks, heads, half),
            (starts, query, d_out, keys[half], keys[1 - half], incoming),
            [
                shape((REACH * BLK, query.shape[3])),
                shape((2, REACH * BLK, HD), F32),
                shape((2, REACH * BLK, HD)),
            ],
            scratch=[
                pltpu.VMEM((2, 2 * REACH * BLK, HD), BF16),
                pltpu.VMEM((2, 2 * REACH * BLK, HD), F32),
            ],
            limit=20,
            after=after,
        )

    dq_late_first, late_first = late(0, ())
    keys[1], rim = join(1, (late_first,))
    rim_first = to_inner(rim)
    dq_late_second, late_second = late(1, (late_first,))
    dq_early_second, own_second, edge_second = early(1, rim_second, (late_second,))
    back_first = to_outer(edge_second)
    dq_early_first, own_first, edge_first = early(0, rim_first, (edge_second,))
    back_second = to_inner(edge_first)
    d_query = call(
        functools.partial(store_queries, REACH),
        (dq_early_first, dq_late_first, dq_early_second, dq_late_second),
        [shape(query.shape)],
        scratch=[pltpu.SemaphoreType.DMA((4,))],
        out_spec=ANY,
    )[0]

    d_keys, packed = (), ()
    for half, late_part, own_part, back, local in (
        (0, late_first, own_first, back_first, edge_second),
        (1, late_second, own_second, back_second, edge_first),
    ):
        packed = call(
            functools.partial(pack_grads, heads, half),
            (late_part, own_part, back, local),
            [block] * heads,
            scratch=[pltpu.VMEM((2, heads * BLK, HD), F32)],
            after=packed[:1],
        )
        inputs = (packed[0], *[swap(packed[t], t) for t in partners], *d_keys)
        d_keys = call(
            functools.partial(join_grads, heads, half),
            inputs,
            [shape(key.shape), shape(value.shape)],
            scratch=[pltpu.SemaphoreType.DMA((2 * heads,))],
            far=range(heads, len(inputs)),
            out_spec=HBM,
            aliases={heads + i: i for i in range(len(d_keys))},
        )
    d_key, d_value = d_keys
    return d_query, d_key, d_value


def solution(mesh):
    tokens = P("ctx", None, "head", None)
    columns = P("ctx", None, None, "head")
    return jax.shard_map(
        per_device,
        mesh=mesh,
        in_specs=(columns, tokens, tokens, columns, P()),
        out_specs=(columns, tokens, tokens),
        check_vma=False,
    )
```

```python
import functools

import jax
import jax.numpy as jnp
from jax import lax
from jax.experimental import pallas as pl
from jax.experimental.pallas import tpu as pltpu
from jax.sharding import PartitionSpec as P

HD = 128
BLK = 128
REACH = 2
SCALE = HD**-0.5
SCALE_LOG2E = SCALE * 1.4426950408889634
LATE = ((1, 1), (1, 2), (2, 1), (3, 1))
EARLY = ((2, 3), (3, 1))
BF16 = jnp.bfloat16
F32 = jnp.float32
VMEM = pl.BlockSpec(memory_space=pltpu.VMEM)
HBM = pl.BlockSpec(memory_space=pltpu.HBM)
ANY = pl.BlockSpec(memory_space=pl.ANY)


def shape(dims, dtype=BF16):
    return jax.ShapeDtypeStruct(dims, dtype)


def call(body, inputs, outs, scratch=(), flops=0, moved=0, limit=12, far=(), after=(), out_spec=VMEM, aliases=None):
    in_specs = [ANY] * len(after) + [
        HBM if i in far else VMEM for i in range(len(inputs))
    ]
    skip = len(after)
    name = body.func.__name__
    return pl.pallas_call(
        lambda *refs: body(*refs[skip:]),
        out_shape=outs,
        in_specs=in_specs,
        out_specs=[out_spec] * len(outs),
        scratch_shapes=list(scratch),
        input_output_aliases=aliases or {},
        compiler_params=pltpu.CompilerParams(vmem_limit_bytes=limit << 20),
        cost_estimate=pl.CostEstimate(flops=flops, bytes_accessed=moved, transcendentals=0),
        name=name,
    )(*after, *inputs)


def carry(pairs, sems):
    copies = [pltpu.make_async_copy(a, b, sems.at[i]) for i, (a, b) in enumerate(pairs)]
    for copy in copies:
        copy.start()
    for copy in copies:
        copy.wait()


def lanes(index):
    return pl.ds(pl.multiple_of(index * HD, HD), HD)


def rows(index, blocks=1):
    return pl.ds(pl.multiple_of(index * BLK, BLK), blocks * BLK)


def slot_of(half):
    odd = lax.rem(lax.axis_index("ctx"), 2)
    return 1 - odd if half == 0 else odd


def is_last():
    return lax.axis_index("ctx") == lax.axis_size("ctx") - 1


def span_of(half):
    ctx = lax.axis_index("ctx")
    return jnp.where(slot_of(half) == 0, ctx, 2 * lax.axis_size("ctx") - 1 - ctx)


def far_blocks(heads, half, key, value, sends):
    me = lax.axis_index("head")
    return [
        (array.at[0, slot_of(half), :, lanes(me ^ t)], sends[t - 2].at[i])
        for t in range(2, heads)
        for i, array in enumerate((key, value))
    ]


def pack_keys(heads, key, value, own, near, *refs):
    sends, sems = refs[:-1], refs[-1]
    me = lax.axis_index("head")
    pairs = far_blocks(heads, 0, key, value, sends)
    for t, there in enumerate((own, near)):
        for half in range(2):
            for i, array in enumerate((key, value)):
                pairs.append((array.at[0, slot_of(half), :, lanes(me ^ t)], there.at[half, i]))
    carry(pairs, sems)


def fetch_rows(what, query, d_out, query_near, d_out_near, sems):
    half, first_block = what
    there = lambda array: array.at[0, slot_of(half), pl.ds(first_block * BLK, REACH * BLK), :]
    return [
        pltpu.make_async_copy(there(query), query_near, sems.at[0]),
        pltpu.make_async_copy(there(d_out), d_out_near, sems.at[1]),
    ]


def load_queries(heads, what, doc_start, key, value, query, d_out, starts_near, query_near, d_out_near, *refs):
    sends, sems = refs[:-1], refs[-1]
    pairs = far_blocks(heads, 1, key, value, sends) + [(doc_start, starts_near)]
    copies = fetch_rows(what, query, d_out, query_near, d_out_near, sems)
    copies += [pltpu.make_async_copy(here, there, sems.at[2 + i]) for i, (here, there) in enumerate(pairs)]
    for copy in copies:
        copy.start()
    for copy in copies:
        copy.wait()


def while_fetching(what, body, inputs, refs):
    if what is None:
        return body(*inputs, *refs)
    query, d_out, *refs, sems = refs
    outs, near, scratch = refs[: what[2]], refs[what[2] : what[2] + 2], refs[what[2] + 2 :]
    copies = fetch_rows(what[:2], query, d_out, *near, sems)
    for copy in copies:
        copy.start()
    body(*inputs, *outs, *scratch)
    for copy in copies:
        copy.wait()


def join_keys(heads, half, own, near, *refs):
    parts, (span, rim) = refs[: heads - 2], refs[heads - 2 :]
    me = lax.axis_index("head")
    for t in range(heads):
        part = own.at[half] if t == 0 else near.at[half] if t == 1 else parts[t - 2]
        span[0, rows(me ^ t), :] = part[0]
        span[1, rows(me ^ t), :] = part[1]
    rim[...] = span[:, (heads - REACH) * BLK :, :]


def dot(a, b, ca, cb):
    return lax.dot_general(a, b, (((ca,), (cb,)), ((), ())), preferred_element_type=F32)


def products(task):
    n, first, queries, grads, keys, d_queries = task
    count = queries.shape[1] // HD
    window = pl.ds(first * BLK, n * BLK)
    k, v = keys[0, window, :], keys[1, window, :]
    q = jnp.concatenate([queries[:, j * HD : (j + 1) * HD] for j in range(count)], axis=0)
    do = jnp.concatenate([grads[:, j * HD : (j + 1) * HD] for j in range(count)], axis=0)
    return k, q, do, dot(k, q, 1, 1), dot(v, do, 1, 1)


def weigh(task, k, q, do, s, dp):
    n = task[0]
    seen = lax.broadcasted_iota(jnp.int32, (BLK, BLK), 0) <= lax.broadcasted_iota(jnp.int32, (BLK, BLK), 1)
    hide = jnp.where(seen, 0.0, -jnp.inf)
    ps, dss = [], []
    for j in range(s.shape[1] // BLK):
        p_, ds_ = weigh_head(n, hide, s[:, j * BLK : (j + 1) * BLK], dp[:, j * BLK : (j + 1) * BLK])
        ps.append(p_)
        dss.append(ds_)
    return k, q, do, jnp.concatenate(ps, axis=1), jnp.concatenate(dss, axis=1)


def weigh_head(n, hide, s, dp):
    last = s[(n - 1) * BLK :] + hide
    return weigh_all(jnp.concatenate([s[: (n - 1) * BLK], last], axis=0) if n > 1 else last, dp)


def weigh_all(s, dp):
    peak = jnp.max(s, axis=0, keepdims=True)
    w = jnp.exp2((s - peak) * SCALE_LOG2E)
    inverse = 1.0 / jnp.sum(w, axis=0, keepdims=True)
    delta = jnp.sum(w * dp, axis=0, keepdims=True) * inverse
    p = w * inverse
    return p.astype(BF16), (p * (dp - delta)).astype(BF16)


def gather(task, d_keys, k, q, do, p, ds):
    n, first, queries, grads, keys, d_queries = task
    window = pl.ds(first * BLK, n * BLK)
    d_keys[0, window, :] += dot(ds, q, 1, 0) * SCALE
    d_keys[1, window, :] += dot(p, do, 1, 0)
    dq = (dot(k.T, ds, 1, 0) * SCALE).astype(BF16)
    for j in range(dq.shape[1] // BLK):
        d_queries[:, j * HD : (j + 1) * HD] = dq[:, j * BLK : (j + 1) * BLK].T


def pair_grads(a, b, d_keys):
    pa = products(a)
    wa = weigh(a, *pa)
    pb = products(b)
    gather(a, d_keys, *wa)
    wb = weigh(b, *pb)
    gather(b, d_keys, *wb)


def loose_grads(reach, visible, query, d_out, keys, d_query, d_keys):
    group = 4
    steps = query.shape[1] // (group * HD)
    seen_rows = (reach + 1) * BLK

    def step(i, carried):
        b, g = i // steps, lax.rem(i, steps)
        window = rows(b + REACH - reach, reach + 1)
        columns = [lanes(g * group + j) for j in range(group)]
        q = jnp.concatenate([query[rows(b), c] for c in columns], axis=0)
        do = jnp.concatenate([d_out[rows(b), c] for c in columns], axis=0)
        k, v = keys[0, window, :], keys[1, window, :]
        count = jnp.where(b == 0, visible[0], visible[1])
        place = lax.broadcasted_iota(jnp.int32, (seen_rows, BLK), 0)
        token = lax.broadcasted_iota(jnp.int32, (seen_rows, BLK), 1)
        seen = (place >= (reach + 1 - count) * BLK) & (place - reach * BLK <= token)
        hide = jnp.where(seen, 0.0, -jnp.inf)
        s, dp = dot(k, q, 1, 1), dot(v, do, 1, 1)
        p, ds = weigh_all(s + jnp.concatenate([hide] * group, axis=1), dp)
        d_keys[0, window, :] += dot(ds, q, 1, 0) * SCALE
        d_keys[1, window, :] += dot(p, do, 1, 0)
        dq = (dot(k.T, ds, 1, 0) * SCALE).astype(BF16)
        for j, c in enumerate(columns):
            d_query[rows(b), c] = dq[:, j * BLK : (j + 1) * BLK].T
        return carried

    lax.fori_loop(0, 2 * steps, step, 0)


def span_part(fast, reach, first_block, per_span, half, doc_start, query, d_out, keys, d_query, d_keys):
    d_keys[...] = jnp.zeros_like(d_keys)
    spot = lax.broadcasted_iota(jnp.int32, doc_start.shape, 1)
    marks = doc_start[...].astype(F32)
    visible = []
    for b in range(2):
        block = span_of(half) * per_span + first_block + b
        mark = jnp.sum(jnp.where(spot == block, 2 * marks, jnp.where(spot == block - 1, marks, 0.0)))
        visible.append(jnp.where(mark > 1.5, 1, jnp.where(mark > 0.5, 2, 3)))

    def task(b, n):
        return (
            n,
            b + REACH + 1 - n,
            query.at[pl.ds(b * BLK, BLK), :],
            d_out.at[pl.ds(b * BLK, BLK), :],
            keys,
            d_query.at[pl.ds(b * BLK, BLK), :],
        )

    common = [(n, then) for n in range(1, REACH + 2) for then in (1, n + 1) if then <= REACH + 1]
    common = [case for case in common if case in fast]
    chosen = False
    for n, then in common:
        here = (visible[0] == n) & (visible[1] == then)
        chosen = here | chosen

        @pl.when(here)
        def _(n=n, then=then):
            pair_grads(task(0, n), task(1, then), d_keys)

    @pl.when(jnp.logical_not(chosen))
    def _():
        loose_grads(reach, visible, query, d_out, keys, d_query, d_keys)


def late_blocks(per_span, half, what, doc_start, query, d_out, keys, *refs):
    def body(doc_start, query, d_out, keys, d_query, d_keys):
        span_part(LATE, REACH, REACH, per_span, half, doc_start, query, d_out, keys, d_query, d_keys)

    while_fetching(what, body, (doc_start, query, d_out, keys), refs)


def early_blocks(per_span, half, what, doc_start, query, d_out, keys, other, incoming, *refs):
    def body(doc_start, query, d_out, keys, other, incoming, d_query, d_own, d_rim, window, d_window):
        cut = REACH * BLK
        window[:, cut:, :] = keys[:, :cut, :]
        window[:, :cut, :] = incoming[...]
        if half == 1:

            @pl.when(is_last())
            def _():
                window[:, :cut, :] = other[:, (per_span - REACH) * BLK :, :]

        span_part(EARLY, REACH - 1, 0, per_span, half, doc_start, query, d_out, window, d_query, d_window)
        d_rim[...] = d_window[:, :cut, :].astype(BF16)
        d_own[...] = d_window[:, cut:, :]

    while_fetching(what, body, (doc_start, query, d_out, keys, other, incoming), refs)


def store_queries(reach, early_first, late_first, early_second, late_second, d_query, sems):
    pairs = []
    for half, parts in ((0, (early_first, late_first)), (1, (early_second, late_second))):
        for part, start in zip(parts, (0, reach * BLK)):
            pairs.append((part, d_query.at[0, slot_of(half), pl.ds(start, part.shape[0]), :]))
    carry(pairs, sems)


def pack_grads(heads, half, late, own, back, local, *refs):
    sends, total = refs[:-1], refs[-1]
    me = lax.axis_index("head")
    cut = REACH * BLK
    total[...] = late[...]
    total[:, :cut, :] += own[...]
    total[:, (heads - REACH) * BLK :, :] += back[...].astype(F32)
    if half == 0:

        @pl.when(is_last())
        def _():
            total[:, (heads - REACH) * BLK :, :] += local[...].astype(F32)

    for t in range(heads):
        sends[t][...] = total[:, rows(me ^ t), :].astype(BF16)


def join_grads(heads, half, *refs):
    parts, (d_key, d_value, sems) = refs[:heads], refs[-3:]
    me = lax.axis_index("head")
    pairs = []
    for t in range(heads):
        for i, array in enumerate((d_key, d_value)):
            pairs.append((parts[t].at[i], array.at[0, slot_of(half), :, lanes(me ^ t)]))
    carry(pairs, sems)


def per_device(query, key, value, d_out, doc_start):
    ctx_count, heads = lax.axis_size("ctx"), lax.axis_size("head")
    block = shape((2, BLK, HD))
    partners = range(1, heads)
    swap = lambda x, t: lax.ppermute(x, "head", [(i, i ^ t) for i in range(heads)])
    outer = [p for i in range(1, ctx_count - 1, 2) for p in ((i, i + 1), (i + 1, i))]
    inner = [p for i in range(0, ctx_count, 2) for p in ((i, i + 1), (i + 1, i))]
    to_outer = lambda x: lax.ppermute(x, "ctx", outer)
    to_inner = lambda x: lax.ppermute(x, "ctx", inner)

    key, value, query, d_out = (
        pltpu.with_memory_space_constraint(x, pltpu.HBM) for x in (key, value, query, d_out)
    )
    own, near, *sends = call(
        functools.partial(pack_keys, heads),
        (key, value),
        [shape((2, 2, BLK, HD))] * 2 + [block] * (heads - 2),
        scratch=[pltpu.SemaphoreType.DMA((4 + 2 * heads,))],
        far=(0, 1),
    )
    near = swap(near, 1)
    parts = [[swap(sends[t - 2], t) for t in range(2, heads)]]
    starts = pltpu.with_memory_space_constraint(doc_start[None], pltpu.HBM)
    two_blocks = shape((REACH * BLK, query.shape[3]))
    starts, *spans = call(
        functools.partial(load_queries, heads, (0, REACH)),
        (starts, key, value, query, d_out),
        [shape(starts.shape, jnp.int32), two_blocks, two_blocks] + [block] * (heads - 2),
        scratch=[pltpu.SemaphoreType.DMA((2 * heads - 1,))],
        moved=4 * query.size,
        far=range(5),
        after=(own,),
    )
    spans, sends = spans[:2], spans[2:]
    parts.append([swap(sends[t - 2], t) for t in range(2, heads)])

    def join(half, after):
        return call(
            functools.partial(join_keys, heads, half),
            (own, near, *parts[half]),
            [shape((2, heads * BLK, HD)), shape((2, REACH * BLK, HD))],
            after=after,
        )

    keys = [None, None]
    keys[0], rim = join(0, (spans[0],))
    rim_second = to_outer(rim)

    def grads(body, half, spans, more, outs, then, after, scratch=()):
        inputs = (starts, *spans, keys[half], *more)
        what = None
        if then is not None:
            what = (*then, len(outs))
            far = (len(inputs), len(inputs) + 1)
            inputs, outs = (*inputs, query, d_out), [*outs, two_blocks, two_blocks]
            scratch = [*scratch, pltpu.SemaphoreType.DMA((2,))]
        return call(
            functools.partial(body, heads, half, what),
            inputs,
            outs,
            scratch=scratch,
            far=() if what is None else far,
            limit=20,
            after=after,
        )

    def late(half, spans, then, after):
        outs = [two_blocks, shape((2, heads * BLK, HD), F32)]
        return grads(late_blocks, half, spans, (), outs, then, after)

    def early(half, spans, incoming, then, after):
        outs = [two_blocks, shape((2, REACH * BLK, HD), F32), shape((2, REACH * BLK, HD))]
        window = (2, 2 * REACH * BLK, HD)
        scratch = [pltpu.VMEM(window, BF16), pltpu.VMEM(window, F32)]
        return grads(early_blocks, half, spans, (keys[1 - half], incoming), outs, then, after, scratch)

    dq_late_first, late_first, *spans = late(0, spans, (1, REACH), ())
    keys[1], rim = join(1, (late_first,))
    rim_first = to_inner(rim)
    dq_late_second, late_second, *spans = late(1, spans, (1, 0), (late_first,))
    dq_early_second, own_second, edge_second, *spans = early(1, spans, rim_second, (0, 0), (late_second,))
    back_first = to_outer(edge_second)
    dq_early_first, own_first, edge_first = early(0, spans, rim_first, None, (edge_second,))
    back_second = to_inner(edge_first)
    d_query = call(
        functools.partial(store_queries, REACH),
        (dq_early_first, dq_late_first, dq_early_second, dq_late_second),
        [shape(query.shape)],
        scratch=[pltpu.SemaphoreType.DMA((4,))],
        out_spec=ANY,
    )[0]

    d_keys, packed = (), ()
    for half, late_part, own_part, back, local in (
        (0, late_first, own_first, back_first, edge_second),
        (1, late_second, own_second, back_second, edge_first),
    ):
        packed = call(
            functools.partial(pack_grads, heads, half),
            (late_part, own_part, back, local),
            [block] * heads,
            scratch=[pltpu.VMEM((2, heads * BLK, HD), F32)],
            after=packed[:1],
        )
        inputs = (packed[0], *[swap(packed[t], t) for t in partners], *d_keys)
        d_keys = call(
            functools.partial(join_grads, heads, half),
            inputs,
            [shape(key.shape), shape(value.shape)],
            scratch=[pltpu.SemaphoreType.DMA((2 * heads,))],
            far=range(heads, len(inputs)),
            out_spec=HBM,
            aliases={heads + i: i for i in range(len(d_keys))},
        )
    d_key, d_value = d_keys
    return d_query, d_key, d_value


def solution(mesh):
    tokens = P("ctx", None, "head", None)
    columns = P("ctx", None, None, "head")
    return jax.shard_map(
        per_device,
        mesh=mesh,
        in_specs=(columns, tokens, tokens, columns, P()),
        out_specs=(columns, tokens, tokens),
        check_vma=False,
    )
```

```python
import functools

import jax
import jax.numpy as jnp
from jax import lax
from jax.experimental import pallas as pl
from jax.experimental.pallas import tpu as pltpu
from jax.sharding import PartitionSpec as P

HD = 128
BLK = 128
REACH = 2
SCALE = HD**-0.5
SCALE_LOG2E = SCALE * 1.4426950408889634
LATE = ((1, 1), (1, 2), (2, 1), (3, 1))
EARLY = ((2, 3), (3, 1))
BF16 = jnp.bfloat16
F32 = jnp.float32
VMEM = pl.BlockSpec(memory_space=pltpu.VMEM)
HBM = pl.BlockSpec(memory_space=pltpu.HBM)
ANY = pl.BlockSpec(memory_space=pl.ANY)


def shape(dims, dtype=BF16):
    return jax.ShapeDtypeStruct(dims, dtype)


def call(body, inputs, outs, scratch=(), flops=0, moved=0, limit=12, far=(), after=(), out_spec=VMEM, aliases=None):
    in_specs = [ANY] * len(after) + [
        HBM if i in far else VMEM for i in range(len(inputs))
    ]
    skip = len(after)
    name = body.func.__name__
    return pl.pallas_call(
        lambda *refs: body(*refs[skip:]),
        out_shape=outs,
        in_specs=in_specs,
        out_specs=[out_spec] * len(outs),
        scratch_shapes=list(scratch),
        input_output_aliases=aliases or {},
        compiler_params=pltpu.CompilerParams(vmem_limit_bytes=limit << 20),
        cost_estimate=pl.CostEstimate(flops=flops, bytes_accessed=moved, transcendentals=0),
        name=name,
    )(*after, *inputs)


def carry(pairs, sems):
    copies = [pltpu.make_async_copy(a, b, sems.at[i]) for i, (a, b) in enumerate(pairs)]
    for copy in copies:
        copy.start()
    for copy in copies:
        copy.wait()


def lanes(index):
    return pl.ds(pl.multiple_of(index * HD, HD), HD)


def rows(index, blocks=1):
    return pl.ds(pl.multiple_of(index * BLK, BLK), blocks * BLK)


def slot_of(half):
    odd = lax.rem(lax.axis_index("ctx"), 2)
    return 1 - odd if half == 0 else odd


def is_last():
    return lax.axis_index("ctx") == lax.axis_size("ctx") - 1


def span_of(half):
    ctx = lax.axis_index("ctx")
    return jnp.where(slot_of(half) == 0, ctx, 2 * lax.axis_size("ctx") - 1 - ctx)


def far_blocks(heads, half, key, value, sends):
    me = lax.axis_index("head")
    return [
        (array.at[0, slot_of(half), :, lanes(me ^ t)], sends[t - 2].at[i])
        for t in range(2, heads)
        for i, array in enumerate((key, value))
    ]


def pack_keys(heads, key, value, own, near, *refs):
    sends, sems = refs[:-1], refs[-1]
    me = lax.axis_index("head")
    pairs = far_blocks(heads, 0, key, value, sends)
    for t, there in enumerate((own, near)):
        for half in range(2):
            for i, array in enumerate((key, value)):
                pairs.append((array.at[0, slot_of(half), :, lanes(me ^ t)], there.at[half, i]))
    carry(pairs, sems)


def fetch_rows(what, query, d_out, query_near, d_out_near, sems):
    half, first_block = what
    there = lambda array: array.at[0, slot_of(half), pl.ds(first_block * BLK, REACH * BLK), :]
    return [
        pltpu.make_async_copy(there(query), query_near, sems.at[0]),
        pltpu.make_async_copy(there(d_out), d_out_near, sems.at[1]),
    ]


def load_queries(heads, what, doc_start, key, value, query, d_out, starts_near, query_near, d_out_near, *refs):
    sends, sems = refs[:-1], refs[-1]
    pairs = far_blocks(heads, 1, key, value, sends) + [(doc_start, starts_near)]
    copies = fetch_rows(what, query, d_out, query_near, d_out_near, sems)
    copies += [pltpu.make_async_copy(here, there, sems.at[2 + i]) for i, (here, there) in enumerate(pairs)]
    for copy in copies:
        copy.start()
    for copy in copies:
        copy.wait()


def while_fetching(what, body, inputs, refs):
    if what is None:
        return body(*inputs, *refs)
    query, d_out, *refs, sems = refs
    outs, near, scratch = refs[: what[2]], refs[what[2] : what[2] + 2], refs[what[2] + 2 :]
    copies = fetch_rows(what[:2], query, d_out, *near, sems)
    for copy in copies:
        copy.start()
    body(*inputs, *outs, *scratch)
    for copy in copies:
        copy.wait()


def join_keys(heads, half, own, near, *refs):
    parts, (span, rim) = refs[: heads - 2], refs[heads - 2 :]
    me = lax.axis_index("head")
    for t in range(heads):
        part = own.at[half] if t == 0 else near.at[half] if t == 1 else parts[t - 2]
        span[0, rows(me ^ t), :] = part[0]
        span[1, rows(me ^ t), :] = part[1]
    rim[...] = span[:, (heads - REACH) * BLK :, :]


def dot(a, b, ca, cb):
    return lax.dot_general(a, b, (((ca,), (cb,)), ((), ())), preferred_element_type=F32)


def products(task):
    n, first, queries, grads, keys, put = task
    count = queries.shape[1] // HD
    window = pl.ds(first * BLK, n * BLK)
    k, v = keys[0, window, :], keys[1, window, :]
    q = jnp.concatenate([queries[:, j * HD : (j + 1) * HD] for j in range(count)], axis=0)
    do = jnp.concatenate([grads[:, j * HD : (j + 1) * HD] for j in range(count)], axis=0)
    return k, q, do, dot(k, q, 1, 1), dot(v, do, 1, 1)


def weigh(task, k, q, do, s, dp):
    n = task[0]
    seen = lax.broadcasted_iota(jnp.int32, (BLK, BLK), 0) <= lax.broadcasted_iota(jnp.int32, (BLK, BLK), 1)
    hide = jnp.where(seen, 0.0, -jnp.inf)
    ps, dss = [], []
    for j in range(s.shape[1] // BLK):
        p_, ds_ = weigh_head(n, hide, s[:, j * BLK : (j + 1) * BLK], dp[:, j * BLK : (j + 1) * BLK])
        ps.append(p_)
        dss.append(ds_)
    return k, q, do, jnp.concatenate(ps, axis=1), jnp.concatenate(dss, axis=1)


def weigh_head(n, hide, s, dp):
    last = s[(n - 1) * BLK :] + hide
    return weigh_all(jnp.concatenate([s[: (n - 1) * BLK], last], axis=0) if n > 1 else last, dp)


def weigh_all(s, dp):
    peak = jnp.max(s, axis=0, keepdims=True)
    w = jnp.exp2((s - peak) * SCALE_LOG2E)
    inverse = 1.0 / jnp.sum(w, axis=0, keepdims=True)
    delta = jnp.sum(w * dp, axis=0, keepdims=True) * inverse
    p = w * inverse
    return p.astype(BF16), (p * (dp - delta)).astype(BF16)


def turn_back(k, ds):
    return (dot(k.T, ds, 1, 0) * SCALE).astype(BF16)


def put_queries(d_queries, k, ds):
    dq = turn_back(k, ds)
    for j in range(dq.shape[1] // BLK):
        d_queries[:, j * HD : (j + 1) * HD] = dq[:, j * BLK : (j + 1) * BLK].T


def gather(task, d_keys, k, q, do, p, ds):
    n, first, queries, grads, keys, put = task
    window = pl.ds(first * BLK, n * BLK)
    d_keys[0, window, :] += dot(ds, q, 1, 0) * SCALE
    d_keys[1, window, :] += dot(p, do, 1, 0)
    put(k, ds)


def pair_grads(a, b, d_keys):
    pa = products(a)
    wa = weigh(a, *pa)
    pb = products(b)
    gather(a, d_keys, *wa)
    wb = weigh(b, *pb)
    gather(b, d_keys, *wb)


def loose_grads(reach, visible, query, d_out, keys, put_loose, d_keys):
    group = 4
    steps = query.shape[1] // (group * HD)
    seen_rows = (reach + 1) * BLK

    def step(i, carried):
        b, g = i // steps, lax.rem(i, steps)
        window = rows(b + REACH - reach, reach + 1)
        columns = [lanes(g * group + j) for j in range(group)]
        q = jnp.concatenate([query[rows(b), c] for c in columns], axis=0)
        do = jnp.concatenate([d_out[rows(b), c] for c in columns], axis=0)
        k, v = keys[0, window, :], keys[1, window, :]
        count = jnp.where(b == 0, visible[0], visible[1])
        place = lax.broadcasted_iota(jnp.int32, (seen_rows, BLK), 0)
        token = lax.broadcasted_iota(jnp.int32, (seen_rows, BLK), 1)
        seen = (place >= (reach + 1 - count) * BLK) & (place - reach * BLK <= token)
        hide = jnp.where(seen, 0.0, -jnp.inf)
        s, dp = dot(k, q, 1, 1), dot(v, do, 1, 1)
        p, ds = weigh_all(s + jnp.concatenate([hide] * group, axis=1), dp)
        d_keys[0, window, :] += dot(ds, q, 1, 0) * SCALE
        d_keys[1, window, :] += dot(p, do, 1, 0)
        put_loose(b, columns, k, ds)
        return carried

    lax.fori_loop(0, 2 * steps, step, 0)


def visible_counts(per_span, half, first_block, doc_start):
    spot = lax.broadcasted_iota(jnp.int32, doc_start.shape, 1)
    marks = doc_start[...].astype(F32)
    visible = []
    for b in range(2):
        block = span_of(half) * per_span + first_block + b
        mark = jnp.sum(jnp.where(spot == block, 2 * marks, jnp.where(spot == block - 1, marks, 0.0)))
        visible.append(jnp.where(mark > 1.5, 1, jnp.where(mark > 0.5, 2, 3)))
    return visible


def span_part(fast, reach, first_block, per_span, half, doc_start, query, d_out, keys, put, put_loose, d_keys):
    d_keys[...] = jnp.zeros_like(d_keys)
    visible = visible_counts(per_span, half, first_block, doc_start)

    def task(b, n):
        return (
            n,
            b + REACH + 1 - n,
            query.at[pl.ds(b * BLK, BLK), :],
            d_out.at[pl.ds(b * BLK, BLK), :],
            keys,
            put(b),
        )

    common = [(n, then) for n in range(1, REACH + 2) for then in (1, n + 1) if then <= REACH + 1]
    common = [case for case in common if case in fast]
    chosen = False
    for n, then in common:
        here = (visible[0] == n) & (visible[1] == then)
        chosen = here | chosen

        @pl.when(here)
        def _(n=n, then=then):
            pair_grads(task(0, n), task(1, then), d_keys)

    @pl.when(jnp.logical_not(chosen))
    def _():
        loose_grads(reach, visible, query, d_out, keys, put_loose, d_keys)


def late_blocks(per_span, half, what, doc_start, query, d_out, keys, *refs):
    def body(doc_start, query, d_out, keys, d_query, d_keys):
        def put(b):
            return functools.partial(put_queries, d_query.at[pl.ds(b * BLK, BLK), :])

        def put_loose(b, columns, k, ds):
            dq = turn_back(k, ds)
            for j, c in enumerate(columns):
                d_query[rows(b), c] = dq[:, j * BLK : (j + 1) * BLK].T

        span_part(LATE, REACH, REACH, per_span, half, doc_start, query, d_out, keys, put, put_loose, d_keys)

    while_fetching(what, body, (doc_start, query, d_out, keys), refs)


def fill_window(per_span, half, window, keys, other, incoming):
    cut = REACH * BLK
    window[:, cut:, :] = keys[:, :cut, :]
    window[:, :cut, :] = incoming[...]
    if half == 1:

        @pl.when(is_last())
        def _():
            window[:, :cut, :] = other[:, (per_span - REACH) * BLK :, :]


def early_blocks(per_span, half, what, doc_start, query, d_out, keys, other, incoming, *refs):
    def body(doc_start, query, d_out, keys, other, incoming, dscores, d_own, d_rim, window, d_window):
        def put(b):
            def store(k, ds):
                dscores[b, : ds.shape[0], :] = ds

            return store

        def put_loose(b, columns, k, ds):
            for j, c in enumerate(columns):
                dscores[b, : ds.shape[0], c] = ds[:, j * BLK : (j + 1) * BLK]

        cut = REACH * BLK
        fill_window(per_span, half, window, keys, other, incoming)
        span_part(EARLY, REACH - 1, 0, per_span, half, doc_start, query, d_out, window, put, put_loose, d_window)
        d_rim[...] = d_window[:, :cut, :].astype(BF16)
        d_own[...] = d_window[:, cut:, :]

    while_fetching(what, body, (doc_start, query, d_out, keys, other, incoming), refs)


def early_queries(per_span, half, doc_start, keys, other, incoming, dscores, d_query, window):
    visible = visible_counts(per_span, half, 0, doc_start)
    fill_window(per_span, half, window, keys, other, incoming)

    def put(counts):
        for b, n in enumerate(counts):
            k = window[0, (b + REACH + 1 - n) * BLK : (b + REACH + 1) * BLK, :]
            put_queries(d_query.at[pl.ds(b * BLK, BLK), :], k, dscores[b, : n * BLK, :])

    chosen = False
    for case in EARLY:
        here = (visible[0] == case[0]) & (visible[1] == case[1])
        chosen = here | chosen
        pl.when(here)(functools.partial(put, case))
    pl.when(jnp.logical_not(chosen))(functools.partial(put, (REACH, REACH)))


def store_queries(reach, early_first, late_first, early_second, late_second, d_query, sems):
    pairs = []
    for half, parts in ((0, (early_first, late_first)), (1, (early_second, late_second))):
        for part, start in zip(parts, (0, reach * BLK)):
            pairs.append((part, d_query.at[0, slot_of(half), pl.ds(start, part.shape[0]), :]))
    carry(pairs, sems)


def pack_grads(heads, half, late, own, back, local, *refs):
    sends, total = refs[:-1], refs[-1]
    me = lax.axis_index("head")
    cut = REACH * BLK
    total[...] = late[...]
    total[:, :cut, :] += own[...]
    total[:, (heads - REACH) * BLK :, :] += back[...].astype(F32)
    if half == 0:

        @pl.when(is_last())
        def _():
            total[:, (heads - REACH) * BLK :, :] += local[...].astype(F32)

    for t in range(heads):
        sends[t][...] = total[:, rows(me ^ t), :].astype(BF16)


def join_grads(heads, half, *refs):
    parts, (d_key, d_value, sems) = refs[:heads], refs[-3:]
    me = lax.axis_index("head")
    pairs = []
    for t in range(heads):
        for i, array in enumerate((d_key, d_value)):
            pairs.append((parts[t].at[i], array.at[0, slot_of(half), :, lanes(me ^ t)]))
    carry(pairs, sems)


def per_device(query, key, value, d_out, doc_start):
    ctx_count, heads = lax.axis_size("ctx"), lax.axis_size("head")
    block = shape((2, BLK, HD))
    partners = range(1, heads)
    swap = lambda x, t: lax.ppermute(x, "head", [(i, i ^ t) for i in range(heads)])
    outer = [p for i in range(1, ctx_count - 1, 2) for p in ((i, i + 1), (i + 1, i))]
    inner = [p for i in range(0, ctx_count, 2) for p in ((i, i + 1), (i + 1, i))]
    to_outer = lambda x: lax.ppermute(x, "ctx", outer)
    to_inner = lambda x: lax.ppermute(x, "ctx", inner)

    key, value, query, d_out = (
        pltpu.with_memory_space_constraint(x, pltpu.HBM) for x in (key, value, query, d_out)
    )
    own, near, *sends = call(
        functools.partial(pack_keys, heads),
        (key, value),
        [shape((2, 2, BLK, HD))] * 2 + [block] * (heads - 2),
        scratch=[pltpu.SemaphoreType.DMA((4 + 2 * heads,))],
        far=(0, 1),
    )
    near = swap(near, 1)
    parts = [[swap(sends[t - 2], t) for t in range(2, heads)]]
    starts = pltpu.with_memory_space_constraint(doc_start[None], pltpu.HBM)
    two_blocks = shape((REACH * BLK, query.shape[3]))
    starts, *spans = call(
        functools.partial(load_queries, heads, (0, REACH)),
        (starts, key, value, query, d_out),
        [shape(starts.shape, jnp.int32), two_blocks, two_blocks] + [block] * (heads - 2),
        scratch=[pltpu.SemaphoreType.DMA((2 * heads - 1,))],
        moved=4 * query.size,
        far=range(5),
        after=(own,),
    )
    spans, sends = spans[:2], spans[2:]
    parts.append([swap(sends[t - 2], t) for t in range(2, heads)])

    def join(half, after):
        return call(
            functools.partial(join_keys, heads, half),
            (own, near, *parts[half]),
            [shape((2, heads * BLK, HD)), shape((2, REACH * BLK, HD))],
            after=after,
        )

    keys = [None, None]
    keys[0], rim = join(0, (spans[0],))
    rim_second = to_outer(rim)

    def grads(body, half, spans, more, outs, then, after, scratch=()):
        inputs = (starts, *spans, keys[half], *more)
        what = None
        if then is not None:
            what = (*then, len(outs))
            far = (len(inputs), len(inputs) + 1)
            inputs, outs = (*inputs, query, d_out), [*outs, two_blocks, two_blocks]
            scratch = [*scratch, pltpu.SemaphoreType.DMA((2,))]
        return call(
            functools.partial(body, heads, half, what),
            inputs,
            outs,
            scratch=scratch,
            far=() if what is None else far,
            limit=20,
            after=after,
        )

    def late(half, spans, then, after):
        outs = [two_blocks, shape((2, heads * BLK, HD), F32)]
        return grads(late_blocks, half, spans, (), outs, then, after)

    def early(half, spans, incoming, then, after):
        dscores = shape((2, (REACH + 1) * BLK, query.shape[3]))
        outs = [dscores, shape((2, REACH * BLK, HD), F32), shape((2, REACH * BLK, HD))]
        window = (2, 2 * REACH * BLK, HD)
        scratch = [pltpu.VMEM(window, BF16), pltpu.VMEM(window, F32)]
        return grads(early_blocks, half, spans, (keys[1 - half], incoming), outs, then, after, scratch)

    dq_late_first, late_first, *spans = late(0, spans, (1, REACH), ())
    keys[1], rim = join(1, (late_first,))
    rim_first = to_inner(rim)
    dq_late_second, late_second, *spans = late(1, spans, (1, 0), (late_first,))
    ds_second, own_second, edge_second, *spans = early(1, spans, rim_second, (0, 0), (late_second,))
    back_first = to_outer(edge_second)
    ds_first, own_first, edge_first = early(0, spans, rim_first, None, (edge_second,))
    back_second = to_inner(edge_first)

    def queries_of(half, incoming, dscores, after):
        return call(
            functools.partial(early_queries, heads, half),
            (starts, keys[half], keys[1 - half], incoming, dscores),
            [two_blocks],
            scratch=[pltpu.VMEM((2, 2 * REACH * BLK, HD), BF16)],
            limit=20,
            after=after,
        )[0]

    dq_early_second = queries_of(1, rim_second, ds_second, (edge_first,))
    dq_early_first = queries_of(0, rim_first, ds_first, (dq_early_second,))
    d_query = call(
        functools.partial(store_queries, REACH),
        (dq_early_first, dq_late_first, dq_early_second, dq_late_second),
        [shape(query.shape)],
        scratch=[pltpu.SemaphoreType.DMA((4,))],
        out_spec=ANY,
    )[0]

    d_keys, packed = (), ()
    for half, late_part, own_part, back, local in (
        (0, late_first, own_first, back_first, edge_second),
        (1, late_second, own_second, back_second, edge_first),
    ):
        packed = call(
            functools.partial(pack_grads, heads, half),
            (late_part, own_part, back, local),
            [block] * heads,
            scratch=[pltpu.VMEM((2, heads * BLK, HD), F32)],
            after=packed[:1],
        )
        inputs = (packed[0], *[swap(packed[t], t) for t in partners], *d_keys)
        d_keys = call(
            functools.partial(join_grads, heads, half),
            inputs,
            [shape(key.shape), shape(value.shape)],
            scratch=[pltpu.SemaphoreType.DMA((2 * heads,))],
            far=range(heads, len(inputs)),
            out_spec=HBM,
            aliases={heads + i: i for i in range(len(d_keys))},
        )
    d_key, d_value = d_keys
    return d_query, d_key, d_value


def solution(mesh):
    tokens = P("ctx", None, "head", None)
    columns = P("ctx", None, None, "head")
    return jax.shard_map(
        per_device,
        mesh=mesh,
        in_specs=(columns, tokens, tokens, columns, P()),
        out_specs=(columns, tokens, tokens),
        check_vma=False,
    )
```

```python
import functools

import jax
import jax.numpy as jnp
from jax import lax
from jax.experimental import pallas as pl
from jax.experimental.pallas import tpu as pltpu
from jax.sharding import PartitionSpec as P

HD = 128
BLK = 128
REACH = 2
SCALE = HD**-0.5
SCALE_LOG2E = SCALE * 1.4426950408889634
LATE = ((1, 1), (1, 2), (2, 1), (3, 1))
EARLY = ((2, 3), (3, 1))
BF16 = jnp.bfloat16
F32 = jnp.float32
VMEM = pl.BlockSpec(memory_space=pltpu.VMEM)
HBM = pl.BlockSpec(memory_space=pltpu.HBM)
ANY = pl.BlockSpec(memory_space=pl.ANY)


def shape(dims, dtype=BF16):
    return jax.ShapeDtypeStruct(dims, dtype)


def call(body, inputs, outs, scratch=(), flops=0, moved=0, limit=12, far=(), after=(), out_spec=VMEM, aliases=None):
    in_specs = [ANY] * len(after) + [
        HBM if i in far else VMEM for i in range(len(inputs))
    ]
    skip = len(after)
    name = body.func.__name__
    return pl.pallas_call(
        lambda *refs: body(*refs[skip:]),
        out_shape=outs,
        in_specs=in_specs,
        out_specs=[out_spec] * len(outs),
        scratch_shapes=list(scratch),
        input_output_aliases=aliases or {},
        compiler_params=pltpu.CompilerParams(vmem_limit_bytes=limit << 20),
        cost_estimate=pl.CostEstimate(flops=flops, bytes_accessed=moved, transcendentals=0),
        name=name,
    )(*after, *inputs)


def carry(pairs, sems):
    copies = [pltpu.make_async_copy(a, b, sems.at[i]) for i, (a, b) in enumerate(pairs)]
    for copy in copies:
        copy.start()
    for copy in copies:
        copy.wait()


def lanes(index):
    return pl.ds(pl.multiple_of(index * HD, HD), HD)


def rows(index, blocks=1):
    return pl.ds(pl.multiple_of(index * BLK, BLK), blocks * BLK)


def slot_of(half):
    odd = lax.rem(lax.axis_index("ctx"), 2)
    return 1 - odd if half == 0 else odd


def is_last():
    return lax.axis_index("ctx") == lax.axis_size("ctx") - 1


def span_of(half):
    ctx = lax.axis_index("ctx")
    return jnp.where(slot_of(half) == 0, ctx, 2 * lax.axis_size("ctx") - 1 - ctx)


def far_blocks(heads, half, key, value, sends):
    me = lax.axis_index("head")
    return [
        (array.at[0, slot_of(half), :, lanes(me ^ t)], sends[t - 2].at[i])
        for t in range(2, heads)
        for i, array in enumerate((key, value))
    ]


def pack_keys(heads, key, value, own, near, *refs):
    sends, sems = refs[:-1], refs[-1]
    me = lax.axis_index("head")
    pairs = far_blocks(heads, 0, key, value, sends)
    for t, there in enumerate((own, near)):
        for half in range(2):
            for i, array in enumerate((key, value)):
                pairs.append((array.at[0, slot_of(half), :, lanes(me ^ t)], there.at[half, i]))
    carry(pairs, sems)


def fetch_rows(what, query, d_out, query_near, d_out_near, sems):
    half, first_block = what
    there = lambda array: array.at[0, slot_of(half), pl.ds(first_block * BLK, REACH * BLK), :]
    return [
        pltpu.make_async_copy(there(query), query_near, sems.at[0]),
        pltpu.make_async_copy(there(d_out), d_out_near, sems.at[1]),
    ]


def load_queries(heads, what, doc_start, key, value, query, d_out, starts_near, query_near, d_out_near, *refs):
    sends, sems = refs[:-1], refs[-1]
    pairs = far_blocks(heads, 1, key, value, sends) + [(doc_start, starts_near)]
    copies = fetch_rows(what, query, d_out, query_near, d_out_near, sems)
    copies += [pltpu.make_async_copy(here, there, sems.at[2 + i]) for i, (here, there) in enumerate(pairs)]
    for copy in copies:
        copy.start()
    for copy in copies:
        copy.wait()


def while_fetching(what, body, inputs, refs):
    if what is None:
        return body(*inputs, *refs)
    query, d_out, *refs, sems = refs
    outs, near, scratch = refs[: what[2]], refs[what[2] : what[2] + 2], refs[what[2] + 2 :]
    copies = fetch_rows(what[:2], query, d_out, *near, sems)
    for copy in copies:
        copy.start()
    body(*inputs, *outs, *scratch)
    for copy in copies:
        copy.wait()


def join_keys(heads, half, own, near, *refs):
    parts, (span, rim) = refs[: heads - 2], refs[heads - 2 :]
    me = lax.axis_index("head")
    for t in range(heads):
        part = own.at[half] if t == 0 else near.at[half] if t == 1 else parts[t - 2]
        span[0, rows(me ^ t), :] = part[0]
        span[1, rows(me ^ t), :] = part[1]
    rim[...] = span[:, (heads - REACH) * BLK :, :]


def dot(a, b, ca, cb):
    return lax.dot_general(a, b, (((ca,), (cb,)), ((), ())), preferred_element_type=F32)


def products(task):
    n, first, queries, grads, keys, put = task
    count = queries.shape[1] // HD
    window = pl.ds(first * BLK, n * BLK)
    k, v = keys[0, window, :], keys[1, window, :]
    q = jnp.concatenate([queries[:, j * HD : (j + 1) * HD] for j in range(count)], axis=0)
    do = jnp.concatenate([grads[:, j * HD : (j + 1) * HD] for j in range(count)], axis=0)
    return k, q, do, dot(k, q, 1, 1), dot(v, do, 1, 1)


def weigh(task, k, q, do, s, dp):
    n = task[0]
    seen = lax.broadcasted_iota(jnp.int32, (BLK, BLK), 0) <= lax.broadcasted_iota(jnp.int32, (BLK, BLK), 1)
    hide = jnp.where(seen, 0.0, -jnp.inf)
    ps, dss = [], []
    for j in range(s.shape[1] // BLK):
        p_, ds_ = weigh_head(n, hide, s[:, j * BLK : (j + 1) * BLK], dp[:, j * BLK : (j + 1) * BLK])
        ps.append(p_)
        dss.append(ds_)
    return k, q, do, jnp.concatenate(ps, axis=1), jnp.concatenate(dss, axis=1)


def weigh_head(n, hide, s, dp):
    last = s[(n - 1) * BLK :] + hide
    return weigh_all(jnp.concatenate([s[: (n - 1) * BLK], last], axis=0) if n > 1 else last, dp)


def weigh_all(s, dp):
    peak = jnp.max(s, axis=0, keepdims=True)
    w = jnp.exp2((s - peak) * SCALE_LOG2E)
    inverse = 1.0 / jnp.sum(w, axis=0, keepdims=True)
    delta = jnp.sum(w * dp, axis=0, keepdims=True) * inverse
    p = w * inverse
    return p.astype(BF16), (p * (dp - delta)).astype(BF16)


def turn_back(k, ds):
    return (dot(k.T, ds, 1, 0) * SCALE).astype(BF16)


def put_queries(d_queries, k, ds):
    dq = turn_back(k, ds)
    for j in range(dq.shape[1] // BLK):
        d_queries[:, j * HD : (j + 1) * HD] = dq[:, j * BLK : (j + 1) * BLK].T


def gather(task, d_keys, k, q, do, p, ds):
    n, first, queries, grads, keys, put = task
    window = pl.ds(first * BLK, n * BLK)
    d_keys[0, window, :] += dot(ds, q, 1, 0) * SCALE
    d_keys[1, window, :] += dot(p, do, 1, 0)
    put(k, ds)


def pair_grads(a, b, d_keys):
    pa = products(a)
    wa = weigh(a, *pa)
    pb = products(b)
    gather(a, d_keys, *wa)
    wb = weigh(b, *pb)
    gather(b, d_keys, *wb)


def loose_grads(reach, visible, query, d_out, keys, put_loose, d_keys):
    group = 4
    steps = query.shape[1] // (group * HD)
    seen_rows = (reach + 1) * BLK

    def step(i, carried):
        b, g = i // steps, lax.rem(i, steps)
        window = rows(b + REACH - reach, reach + 1)
        columns = [lanes(g * group + j) for j in range(group)]
        q = jnp.concatenate([query[rows(b), c] for c in columns], axis=0)
        do = jnp.concatenate([d_out[rows(b), c] for c in columns], axis=0)
        k, v = keys[0, window, :], keys[1, window, :]
        count = jnp.where(b == 0, visible[0], visible[1])
        place = lax.broadcasted_iota(jnp.int32, (seen_rows, BLK), 0)
        token = lax.broadcasted_iota(jnp.int32, (seen_rows, BLK), 1)
        seen = (place >= (reach + 1 - count) * BLK) & (place - reach * BLK <= token)
        hide = jnp.where(seen, 0.0, -jnp.inf)
        s, dp = dot(k, q, 1, 1), dot(v, do, 1, 1)
        p, ds = weigh_all(s + jnp.concatenate([hide] * group, axis=1), dp)
        d_keys[0, window, :] += dot(ds, q, 1, 0) * SCALE
        d_keys[1, window, :] += dot(p, do, 1, 0)
        put_loose(b, columns, k, ds)
        return carried

    lax.fori_loop(0, 2 * steps, step, 0)


def visible_counts(per_span, half, first_block, doc_start):
    spot = lax.broadcasted_iota(jnp.int32, doc_start.shape, 1)
    marks = doc_start[...].astype(F32)
    visible = []
    for b in range(2):
        block = span_of(half) * per_span + first_block + b
        mark = jnp.sum(jnp.where(spot == block, 2 * marks, jnp.where(spot == block - 1, marks, 0.0)))
        visible.append(jnp.where(mark > 1.5, 1, jnp.where(mark > 0.5, 2, 3)))
    return visible


def span_part(fast, reach, first_block, per_span, half, doc_start, query, d_out, keys, put, put_loose, d_keys):
    d_keys[...] = jnp.zeros_like(d_keys)
    visible = visible_counts(per_span, half, first_block, doc_start)

    def task(b, n):
        return (
            n,
            b + REACH + 1 - n,
            query.at[pl.ds(b * BLK, BLK), :],
            d_out.at[pl.ds(b * BLK, BLK), :],
            keys,
            put(b),
        )

    common = [(n, then) for n in range(1, REACH + 2) for then in (1, n + 1) if then <= REACH + 1]
    common = [case for case in common if case in fast]
    chosen = False
    for n, then in common:
        here = (visible[0] == n) & (visible[1] == then)
        chosen = here | chosen

        @pl.when(here)
        def _(n=n, then=then):
            pair_grads(task(0, n), task(1, then), d_keys)

    @pl.when(jnp.logical_not(chosen))
    def _():
        loose_grads(reach, visible, query, d_out, keys, put_loose, d_keys)


def keepers(dscores):
    def put(b):
        def store(k, ds):
            dscores[b, : ds.shape[0], :] = ds

        return store

    def put_loose(b, columns, k, ds):
        for j, c in enumerate(columns):
            dscores[b, : ds.shape[0], c] = ds[:, j * BLK : (j + 1) * BLK]

    return put, put_loose


def late_blocks(per_span, half, what, doc_start, query, d_out, keys, *refs):
    def body(doc_start, query, d_out, keys, kept, d_keys):
        def put(b):
            return functools.partial(put_queries, kept.at[pl.ds(b * BLK, BLK), :])

        def put_loose(b, columns, k, ds):
            dq = turn_back(k, ds)
            for j, c in enumerate(columns):
                kept[rows(b), c] = dq[:, j * BLK : (j + 1) * BLK].T

        writers = (put, put_loose) if half == 0 else keepers(kept)
        span_part(LATE, REACH, REACH, per_span, half, doc_start, query, d_out, keys, *writers, d_keys)

    while_fetching(what, body, (doc_start, query, d_out, keys), refs)


def fill_window(per_span, half, window, keys, other, incoming):
    cut = REACH * BLK
    window[:, cut:, :] = keys[:, :cut, :]
    window[:, :cut, :] = incoming[...]
    if half == 1:

        @pl.when(is_last())
        def _():
            window[:, :cut, :] = other[:, (per_span - REACH) * BLK :, :]


def early_blocks(per_span, half, what, doc_start, query, d_out, keys, other, incoming, *refs):
    def body(doc_start, query, d_out, keys, other, incoming, dscores, d_own, d_rim, window, d_window):
        cut = REACH * BLK
        fill_window(per_span, half, window, keys, other, incoming)
        span_part(EARLY, REACH - 1, 0, per_span, half, doc_start, query, d_out, window, *keepers(dscores), d_window)
        d_rim[...] = d_window[:, :cut, :].astype(BF16)
        d_own[...] = d_window[:, cut:, :]

    while_fetching(what, body, (doc_start, query, d_out, keys, other, incoming), refs)


def finish_queries(per_span, doc_start, late_first, keys_0, keys_1, rim_second, rim_first, *refs):
    ds_late, ds_second, ds_first, d_query, part_late, part_second, part_first, window, sems = refs
    copies = []

    def send(part, half, first_block):
        there = d_query.at[0, slot_of(half), pl.ds(first_block * BLK, REACH * BLK), :]
        copies.append(pltpu.make_async_copy(part, there, sems.at[len(copies)]))
        copies[-1].start()

    def work_out(fast, reach, half, first_block, keys, dscores, part):
        visible = visible_counts(per_span, half, first_block, doc_start)

        def put(counts):
            for b, n in enumerate(counts):
                k = keys[0, (b + REACH + 1 - n) * BLK : (b + REACH + 1) * BLK, :]
                put_queries(part.at[pl.ds(b * BLK, BLK), :], k, dscores[b, : n * BLK, :])

        chosen = False
        for case in fast:
            here = (visible[0] == case[0]) & (visible[1] == case[1])
            chosen = here | chosen
            pl.when(here)(functools.partial(put, case))
        pl.when(jnp.logical_not(chosen))(functools.partial(put, (reach + 1, reach + 1)))
        send(part, half, first_block)

    send(late_first, 0, REACH)
    work_out(LATE, REACH, 1, REACH, keys_1, ds_late, part_late)
    fill_window(per_span, 1, window, keys_1, keys_0, rim_second)
    work_out(EARLY, REACH - 1, 1, 0, window, ds_second, part_second)
    fill_window(per_span, 0, window, keys_0, keys_1, rim_first)
    work_out(EARLY, REACH - 1, 0, 0, window, ds_first, part_first)
    for copy in copies:
        copy.wait()


def pack_grads(heads, half, late, own, back, local, *refs):
    sends, total = refs[:-1], refs[-1]
    me = lax.axis_index("head")
    cut = REACH * BLK
    total[...] = late[...]
    total[:, :cut, :] += own[...]
    total[:, (heads - REACH) * BLK :, :] += back[...].astype(F32)
    if half == 0:

        @pl.when(is_last())
        def _():
            total[:, (heads - REACH) * BLK :, :] += local[...].astype(F32)

    for t in range(heads):
        sends[t][...] = total[:, rows(me ^ t), :].astype(BF16)


def join_grads(heads, half, *refs):
    parts, (d_key, d_value, sems) = refs[:heads], refs[-3:]
    me = lax.axis_index("head")
    pairs = []
    for t in range(heads):
        for i, array in enumerate((d_key, d_value)):
            pairs.append((parts[t].at[i], array.at[0, slot_of(half), :, lanes(me ^ t)]))
    carry(pairs, sems)


def per_device(query, key, value, d_out, doc_start):
    ctx_count, heads = lax.axis_size("ctx"), lax.axis_size("head")
    block = shape((2, BLK, HD))
    partners = range(1, heads)
    swap = lambda x, t: lax.ppermute(x, "head", [(i, i ^ t) for i in range(heads)])
    outer = [p for i in range(1, ctx_count - 1, 2) for p in ((i, i + 1), (i + 1, i))]
    inner = [p for i in range(0, ctx_count, 2) for p in ((i, i + 1), (i + 1, i))]
    to_outer = lambda x: lax.ppermute(x, "ctx", outer)
    to_inner = lambda x: lax.ppermute(x, "ctx", inner)

    key, value, query, d_out = (
        pltpu.with_memory_space_constraint(x, pltpu.HBM) for x in (key, value, query, d_out)
    )
    own, near, *sends = call(
        functools.partial(pack_keys, heads),
        (key, value),
        [shape((2, 2, BLK, HD))] * 2 + [block] * (heads - 2),
        scratch=[pltpu.SemaphoreType.DMA((4 + 2 * heads,))],
        far=(0, 1),
    )
    near = swap(near, 1)
    parts = [[swap(sends[t - 2], t) for t in range(2, heads)]]
    starts = pltpu.with_memory_space_constraint(doc_start[None], pltpu.HBM)
    two_blocks = shape((REACH * BLK, query.shape[3]))
    starts, *spans = call(
        functools.partial(load_queries, heads, (0, REACH)),
        (starts, key, value, query, d_out),
        [shape(starts.shape, jnp.int32), two_blocks, two_blocks] + [block] * (heads - 2),
        scratch=[pltpu.SemaphoreType.DMA((2 * heads - 1,))],
        moved=4 * query.size,
        far=range(5),
        after=(own,),
    )
    spans, sends = spans[:2], spans[2:]
    parts.append([swap(sends[t - 2], t) for t in range(2, heads)])

    def join(half, after):
        return call(
            functools.partial(join_keys, heads, half),
            (own, near, *parts[half]),
            [shape((2, heads * BLK, HD)), shape((2, REACH * BLK, HD))],
            after=after,
        )

    keys = [None, None]
    keys[0], rim = join(0, (spans[0],))
    rim_second = to_outer(rim)

    def grads(body, half, spans, more, outs, then, after, scratch=()):
        inputs = (starts, *spans, keys[half], *more)
        what = None
        if then is not None:
            what = (*then, len(outs))
            far = (len(inputs), len(inputs) + 1)
            inputs, outs = (*inputs, query, d_out), [*outs, two_blocks, two_blocks]
            scratch = [*scratch, pltpu.SemaphoreType.DMA((2,))]
        return call(
            functools.partial(body, heads, half, what),
            inputs,
            outs,
            scratch=scratch,
            far=() if what is None else far,
            limit=20,
            after=after,
        )

    dscores = shape((2, (REACH + 1) * BLK, query.shape[3]))

    def late(half, spans, then, after):
        outs = [two_blocks if half == 0 else dscores, shape((2, heads * BLK, HD), F32)]
        return grads(late_blocks, half, spans, (), outs, then, after)

    def early(half, spans, incoming, then, after):
        outs = [dscores, shape((2, REACH * BLK, HD), F32), shape((2, REACH * BLK, HD))]
        window = (2, 2 * REACH * BLK, HD)
        scratch = [pltpu.VMEM(window, BF16), pltpu.VMEM(window, F32)]
        return grads(early_blocks, half, spans, (keys[1 - half], incoming), outs, then, after, scratch)

    dq_late_first, late_first, *spans = late(0, spans, (1, REACH), ())
    keys[1], rim = join(1, (late_first,))
    rim_first = to_inner(rim)
    ds_late, late_second, *spans = late(1, spans, (1, 0), (late_first,))
    ds_second, own_second, edge_second, *spans = early(1, spans, rim_second, (0, 0), (late_second,))
    back_first = to_outer(edge_second)
    ds_first, own_first, edge_first = early(0, spans, rim_first, None, (edge_second,))
    back_second = to_inner(edge_first)

    part = pltpu.VMEM(two_blocks.shape, BF16)
    d_query = call(
        functools.partial(finish_queries, heads),
        (starts, dq_late_first, *keys, rim_second, rim_first, ds_late, ds_second, ds_first),
        [shape(query.shape)],
        scratch=[part] * 3 + [pltpu.VMEM((2, 2 * REACH * BLK, HD), BF16), pltpu.SemaphoreType.DMA((4,))],
        limit=20,
        out_spec=HBM,
    )[0]

    d_keys, packed = (), ()
    for half, late_part, own_part, back, local in (
        (0, late_first, own_first, back_first, edge_second),
        (1, late_second, own_second, back_second, edge_first),
    ):
        packed = call(
            functools.partial(pack_grads, heads, half),
            (late_part, own_part, back, local),
            [block] * heads,
            scratch=[pltpu.VMEM((2, heads * BLK, HD), F32)],
            after=packed[:1],
        )
        inputs = (packed[0], *[swap(packed[t], t) for t in partners], *d_keys)
        d_keys = call(
            functools.partial(join_grads, heads, half),
            inputs,
            [shape(key.shape), shape(value.shape)],
            scratch=[pltpu.SemaphoreType.DMA((2 * heads,))],
            far=range(heads, len(inputs)),
            out_spec=HBM,
            aliases={heads + i: i for i in range(len(d_keys))},
        )
    d_key, d_value = d_keys
    return d_query, d_key, d_value


def solution(mesh):
    tokens = P("ctx", None, "head", None)
    columns = P("ctx", None, None, "head")
    return jax.shard_map(
        per_device,
        mesh=mesh,
        in_specs=(columns, tokens, tokens, columns, P()),
        out_specs=(columns, tokens, tokens),
        check_vma=False,
    )
```

```python
import functools

import jax
import jax.numpy as jnp
from jax import lax
from jax.experimental import pallas as pl
from jax.experimental.pallas import tpu as pltpu
from jax.sharding import PartitionSpec as P

HD = 128
BLK = 128
REACH = 2
SCALE = HD**-0.5
SCALE_LOG2E = SCALE * 1.4426950408889634
LATE = ((1, 1), (1, 2), (2, 1), (3, 1))
EARLY = ((2, 3), (3, 1))
BF16 = jnp.bfloat16
F32 = jnp.float32
VMEM = pl.BlockSpec(memory_space=pltpu.VMEM)
HBM = pl.BlockSpec(memory_space=pltpu.HBM)
ANY = pl.BlockSpec(memory_space=pl.ANY)


def shape(dims, dtype=BF16):
    return jax.ShapeDtypeStruct(dims, dtype)


def call(body, inputs, outs, scratch=(), flops=0, moved=0, limit=12, far=(), after=(), out_spec=VMEM, aliases=None):
    in_specs = [ANY] * len(after) + [
        HBM if i in far else VMEM for i in range(len(inputs))
    ]
    skip = len(after)
    name = body.func.__name__
    return pl.pallas_call(
        lambda *refs: body(*refs[skip:]),
        out_shape=outs,
        in_specs=in_specs,
        out_specs=[out_spec] * len(outs),
        scratch_shapes=list(scratch),
        input_output_aliases=aliases or {},
        compiler_params=pltpu.CompilerParams(vmem_limit_bytes=limit << 20),
        cost_estimate=pl.CostEstimate(flops=flops, bytes_accessed=moved, transcendentals=0),
        name=name,
    )(*after, *inputs)


def carry(pairs, sems):
    copies = [pltpu.make_async_copy(a, b, sems.at[i]) for i, (a, b) in enumerate(pairs)]
    for copy in copies:
        copy.start()
    for copy in copies:
        copy.wait()


def lanes(index):
    return pl.ds(pl.multiple_of(index * HD, HD), HD)


def rows(index, blocks=1):
    return pl.ds(pl.multiple_of(index * BLK, BLK), blocks * BLK)


def slot_of(half):
    odd = lax.rem(lax.axis_index("ctx"), 2)
    return 1 - odd if half == 0 else odd


def is_last():
    return lax.axis_index("ctx") == lax.axis_size("ctx") - 1


def span_of(half):
    ctx = lax.axis_index("ctx")
    return jnp.where(slot_of(half) == 0, ctx, 2 * lax.axis_size("ctx") - 1 - ctx)


def far_blocks(heads, half, key, value, sends):
    me = lax.axis_index("head")
    return [
        (array.at[0, slot_of(half), :, lanes(me ^ t)], sends[t - 2].at[i])
        for t in range(2, heads)
        for i, array in enumerate((key, value))
    ]


def pack_keys(heads, key, value, own, near, *refs):
    sends, sems = refs[:-1], refs[-1]
    me = lax.axis_index("head")
    pairs = far_blocks(heads, 0, key, value, sends)
    for t, there in enumerate((own, near)):
        for half in range(2):
            for i, array in enumerate((key, value)):
                pairs.append((array.at[0, slot_of(half), :, lanes(me ^ t)], there.at[half, i]))
    carry(pairs, sems)


def fetch_rows(what, query, d_out, query_near, d_out_near, sems):
    half, first_block = what
    there = lambda array: array.at[0, slot_of(half), pl.ds(first_block * BLK, REACH * BLK), :]
    return [
        pltpu.make_async_copy(there(query), query_near, sems.at[0]),
        pltpu.make_async_copy(there(d_out), d_out_near, sems.at[1]),
    ]


def load_queries(heads, what, doc_start, key, value, query, d_out, starts_near, query_near, d_out_near, *refs):
    sends, sems = refs[:-1], refs[-1]
    pairs = far_blocks(heads, 1, key, value, sends) + [(doc_start, starts_near)]
    copies = fetch_rows(what, query, d_out, query_near, d_out_near, sems)
    copies += [pltpu.make_async_copy(here, there, sems.at[2 + i]) for i, (here, there) in enumerate(pairs)]
    for copy in copies:
        copy.start()
    for copy in copies:
        copy.wait()


def while_fetching(what, body, inputs, refs):
    if what is None:
        return body(*inputs, *refs)
    query, d_out, *refs, sems = refs
    outs, near, scratch = refs[: what[2]], refs[what[2] : what[2] + 2], refs[what[2] + 2 :]
    copies = fetch_rows(what[:2], query, d_out, *near, sems)
    for copy in copies:
        copy.start()
    body(*inputs, *outs, *scratch)
    for copy in copies:
        copy.wait()


def join_keys(heads, half, own, near, *refs):
    parts, (span, rim) = refs[: heads - 2], refs[heads - 2 :]
    me = lax.axis_index("head")
    for t in range(heads):
        part = own.at[half] if t == 0 else near.at[half] if t == 1 else parts[t - 2]
        span[0, rows(me ^ t), :] = part[0]
        span[1, rows(me ^ t), :] = part[1]
    rim[...] = span[:, (heads - REACH) * BLK :, :]


def dot(a, b, ca, cb):
    return lax.dot_general(a, b, (((ca,), (cb,)), ((), ())), preferred_element_type=F32)


def products(task):
    n, first, queries, grads, keys, put = task
    count = queries.shape[1] // HD
    window = pl.ds(first * BLK, n * BLK)
    k, v = keys[0, window, :], keys[1, window, :]
    q = jnp.concatenate([queries[:, j * HD : (j + 1) * HD] for j in range(count)], axis=0)
    do = jnp.concatenate([grads[:, j * HD : (j + 1) * HD] for j in range(count)], axis=0)
    return k, q, do, dot(k, q, 1, 1), dot(v, do, 1, 1)


def weigh(task, k, q, do, s, dp):
    n = task[0]
    seen = lax.broadcasted_iota(jnp.int32, (BLK, BLK), 0) <= lax.broadcasted_iota(jnp.int32, (BLK, BLK), 1)
    hide = jnp.where(seen, 0.0, -jnp.inf)
    ps, dss = [], []
    for j in range(s.shape[1] // BLK):
        p_, ds_ = weigh_head(n, hide, s[:, j * BLK : (j + 1) * BLK], dp[:, j * BLK : (j + 1) * BLK])
        ps.append(p_)
        dss.append(ds_)
    return k, q, do, jnp.concatenate(ps, axis=1), jnp.concatenate(dss, axis=1)


def weigh_head(n, hide, s, dp):
    last = s[(n - 1) * BLK :] + hide
    return weigh_all(jnp.concatenate([s[: (n - 1) * BLK], last], axis=0) if n > 1 else last, dp)


def weigh_all(s, dp):
    peak = jnp.max(s, axis=0, keepdims=True)
    w = jnp.exp2((s - peak) * SCALE_LOG2E)
    inverse = 1.0 / jnp.sum(w, axis=0, keepdims=True)
    delta = jnp.sum(w * dp, axis=0, keepdims=True) * inverse
    p = w * inverse
    return p.astype(BF16), (p * (dp - delta)).astype(BF16)


def turn_back(k, ds):
    return (dot(k.T, ds, 1, 0) * SCALE).astype(BF16)


def put_queries(d_queries, k, ds):
    dq = turn_back(k, ds)
    for j in range(dq.shape[1] // BLK):
        d_queries[:, j * HD : (j + 1) * HD] = dq[:, j * BLK : (j + 1) * BLK].T


def gather(task, d_keys, k, q, do, p, ds):
    n, first, queries, grads, keys, put = task
    window = pl.ds(first * BLK, n * BLK)
    d_keys[0, window, :] += dot(ds, q, 1, 0) * SCALE
    d_keys[1, window, :] += dot(p, do, 1, 0)
    put(k, ds)


def pair_grads(a, b, d_keys):
    pa = products(a)
    wa = weigh(a, *pa)
    pb = products(b)
    gather(a, d_keys, *wa)
    wb = weigh(b, *pb)
    gather(b, d_keys, *wb)


def loose_grads(reach, visible, query, d_out, keys, put_loose, d_keys):
    group = 4
    steps = query.shape[1] // (group * HD)
    seen_rows = (reach + 1) * BLK

    def step(i, carried):
        b, g = i // steps, lax.rem(i, steps)
        window = rows(b + REACH - reach, reach + 1)
        columns = [lanes(g * group + j) for j in range(group)]
        q = jnp.concatenate([query[rows(b), c] for c in columns], axis=0)
        do = jnp.concatenate([d_out[rows(b), c] for c in columns], axis=0)
        k, v = keys[0, window, :], keys[1, window, :]
        count = jnp.where(b == 0, visible[0], visible[1])
        place = lax.broadcasted_iota(jnp.int32, (seen_rows, BLK), 0)
        token = lax.broadcasted_iota(jnp.int32, (seen_rows, BLK), 1)
        seen = (place >= (reach + 1 - count) * BLK) & (place - reach * BLK <= token)
        hide = jnp.where(seen, 0.0, -jnp.inf)
        s, dp = dot(k, q, 1, 1), dot(v, do, 1, 1)
        p, ds = weigh_all(s + jnp.concatenate([hide] * group, axis=1), dp)
        d_keys[0, window, :] += dot(ds, q, 1, 0) * SCALE
        d_keys[1, window, :] += dot(p, do, 1, 0)
        put_loose(b, columns, k, ds)
        return carried

    lax.fori_loop(0, 2 * steps, step, 0)


def visible_counts(per_span, half, first_block, doc_start):
    spot = lax.broadcasted_iota(jnp.int32, doc_start.shape, 1)
    marks = doc_start[...].astype(F32)
    visible = []
    for b in range(2):
        block = span_of(half) * per_span + first_block + b
        mark = jnp.sum(jnp.where(spot == block, 2 * marks, jnp.where(spot == block - 1, marks, 0.0)))
        visible.append(jnp.where(mark > 1.5, 1, jnp.where(mark > 0.5, 2, 3)))
    return visible


def span_part(fast, reach, first_block, per_span, half, doc_start, query, d_out, keys, put, put_loose, d_keys):
    d_keys[...] = jnp.zeros_like(d_keys)
    visible = visible_counts(per_span, half, first_block, doc_start)

    def task(b, n):
        return (
            n,
            b + REACH + 1 - n,
            query.at[pl.ds(b * BLK, BLK), :],
            d_out.at[pl.ds(b * BLK, BLK), :],
            keys,
            put(b),
        )

    common = [(n, then) for n in range(1, REACH + 2) for then in (1, n + 1) if then <= REACH + 1]
    common = [case for case in common if case in fast]
    chosen = False
    for n, then in common:
        here = (visible[0] == n) & (visible[1] == then)
        chosen = here | chosen

        @pl.when(here)
        def _(n=n, then=then):
            pair_grads(task(0, n), task(1, then), d_keys)

    @pl.when(jnp.logical_not(chosen))
    def _():
        loose_grads(reach, visible, query, d_out, keys, put_loose, d_keys)


def keepers(dscores):
    def put(b):
        def store(k, ds):
            dscores[b, : ds.shape[0], :] = ds

        return store

    def put_loose(b, columns, k, ds):
        for j, c in enumerate(columns):
            dscores[b, : ds.shape[0], c] = ds[:, j * BLK : (j + 1) * BLK]

    return put, put_loose


def late_blocks(per_span, half, what, doc_start, query, d_out, keys, *refs):
    def body(doc_start, query, d_out, keys, kept, d_keys):
        span_part(LATE, REACH, REACH, per_span, half, doc_start, query, d_out, keys, *keepers(kept), d_keys)

    while_fetching(what, body, (doc_start, query, d_out, keys), refs)


def fill_window(per_span, half, window, keys, other, incoming):
    cut = REACH * BLK
    window[:, cut:, :] = keys[:, :cut, :]
    window[:, :cut, :] = incoming[...]
    if half == 1:

        @pl.when(is_last())
        def _():
            window[:, :cut, :] = other[:, (per_span - REACH) * BLK :, :]


def early_blocks(per_span, half, what, doc_start, query, d_out, keys, other, incoming, *refs):
    def body(doc_start, query, d_out, keys, other, incoming, dscores, d_own, d_rim, window, d_window):
        cut = REACH * BLK
        fill_window(per_span, half, window, keys, other, incoming)
        span_part(EARLY, REACH - 1, 0, per_span, half, doc_start, query, d_out, window, *keepers(dscores), d_window)
        d_rim[...] = d_window[:, :cut, :].astype(BF16)
        d_own[...] = d_window[:, cut:, :]

    while_fetching(what, body, (doc_start, query, d_out, keys, other, incoming), refs)


def finish_queries(per_span, doc_start, keys_0, keys_1, rim_second, rim_first, *refs):
    ds_late_0, ds_late_1, ds_second, ds_first, d_query = refs[:5]
    part_late_0, part_late_1, part_second, part_first, window, sems = refs[5:]
    copies = []

    def send(part, half, first_block):
        there = d_query.at[0, slot_of(half), pl.ds(first_block * BLK, REACH * BLK), :]
        copies.append(pltpu.make_async_copy(part, there, sems.at[len(copies)]))
        copies[-1].start()

    def work_out(fast, reach, half, first_block, keys, dscores, part):
        visible = visible_counts(per_span, half, first_block, doc_start)

        def put(counts):
            for b, n in enumerate(counts):
                k = keys[0, (b + REACH + 1 - n) * BLK : (b + REACH + 1) * BLK, :]
                put_queries(part.at[pl.ds(b * BLK, BLK), :], k, dscores[b, : n * BLK, :])

        chosen = False
        for case in fast:
            here = (visible[0] == case[0]) & (visible[1] == case[1])
            chosen = here | chosen
            pl.when(here)(functools.partial(put, case))
        pl.when(jnp.logical_not(chosen))(functools.partial(put, (reach + 1, reach + 1)))
        send(part, half, first_block)

    work_out(LATE, REACH, 0, REACH, keys_0, ds_late_0, part_late_0)
    work_out(LATE, REACH, 1, REACH, keys_1, ds_late_1, part_late_1)
    fill_window(per_span, 1, window, keys_1, keys_0, rim_second)
    work_out(EARLY, REACH - 1, 1, 0, window, ds_second, part_second)
    fill_window(per_span, 0, window, keys_0, keys_1, rim_first)
    work_out(EARLY, REACH - 1, 0, 0, window, ds_first, part_first)
    for copy in copies:
        copy.wait()


def pack_grads(heads, half, late, own, back, local, *refs):
    sends, total = refs[:-1], refs[-1]
    me = lax.axis_index("head")
    cut = REACH * BLK
    total[...] = late[...]
    total[:, :cut, :] += own[...]
    total[:, (heads - REACH) * BLK :, :] += back[...].astype(F32)
    if half == 0:

        @pl.when(is_last())
        def _():
            total[:, (heads - REACH) * BLK :, :] += local[...].astype(F32)

    for t in range(heads):
        sends[t][...] = total[:, rows(me ^ t), :].astype(BF16)


def join_grads(heads, half, *refs):
    parts, (d_key, d_value, sems) = refs[:heads], refs[-3:]
    me = lax.axis_index("head")
    pairs = []
    for t in range(heads):
        for i, array in enumerate((d_key, d_value)):
            pairs.append((parts[t].at[i], array.at[0, slot_of(half), :, lanes(me ^ t)]))
    carry(pairs, sems)


def per_device(query, key, value, d_out, doc_start):
    ctx_count, heads = lax.axis_size("ctx"), lax.axis_size("head")
    block = shape((2, BLK, HD))
    partners = range(1, heads)
    swap = lambda x, t: lax.ppermute(x, "head", [(i, i ^ t) for i in range(heads)])
    outer = [p for i in range(1, ctx_count - 1, 2) for p in ((i, i + 1), (i + 1, i))]
    inner = [p for i in range(0, ctx_count, 2) for p in ((i, i + 1), (i + 1, i))]
    to_outer = lambda x: lax.ppermute(x, "ctx", outer)
    to_inner = lambda x: lax.ppermute(x, "ctx", inner)

    key, value, query, d_out = (
        pltpu.with_memory_space_constraint(x, pltpu.HBM) for x in (key, value, query, d_out)
    )
    own, near, *sends = call(
        functools.partial(pack_keys, heads),
        (key, value),
        [shape((2, 2, BLK, HD))] * 2 + [block] * (heads - 2),
        scratch=[pltpu.SemaphoreType.DMA((4 + 2 * heads,))],
        far=(0, 1),
    )
    near = swap(near, 1)
    parts = [[swap(sends[t - 2], t) for t in range(2, heads)]]
    starts = pltpu.with_memory_space_constraint(doc_start[None], pltpu.HBM)
    two_blocks = shape((REACH * BLK, query.shape[3]))
    starts, *spans = call(
        functools.partial(load_queries, heads, (0, REACH)),
        (starts, key, value, query, d_out),
        [shape(starts.shape, jnp.int32), two_blocks, two_blocks] + [block] * (heads - 2),
        scratch=[pltpu.SemaphoreType.DMA((2 * heads - 1,))],
        moved=4 * query.size,
        far=range(5),
        after=(own,),
    )
    spans, sends = spans[:2], spans[2:]
    parts.append([swap(sends[t - 2], t) for t in range(2, heads)])

    def join(half, after):
        return call(
            functools.partial(join_keys, heads, half),
            (own, near, *parts[half]),
            [shape((2, heads * BLK, HD)), shape((2, REACH * BLK, HD))],
            after=after,
        )

    keys = [None, None]
    keys[0], rim = join(0, (spans[0],))
    rim_second = to_outer(rim)

    def grads(body, half, spans, more, outs, then, after, scratch=()):
        inputs = (starts, *spans, keys[half], *more)
        what = None
        if then is not None:
            what = (*then, len(outs))
            far = (len(inputs), len(inputs) + 1)
            inputs, outs = (*inputs, query, d_out), [*outs, two_blocks, two_blocks]
            scratch = [*scratch, pltpu.SemaphoreType.DMA((2,))]
        return call(
            functools.partial(body, heads, half, what),
            inputs,
            outs,
            scratch=scratch,
            far=() if what is None else far,
            limit=20,
            after=after,
        )

    dscores = shape((2, (REACH + 1) * BLK, query.shape[3]))

    def late(half, spans, then, after):
        outs = [dscores, shape((2, heads * BLK, HD), F32)]
        return grads(late_blocks, half, spans, (), outs, then, after)

    def early(half, spans, incoming, then, after):
        outs = [dscores, shape((2, REACH * BLK, HD), F32), shape((2, REACH * BLK, HD))]
        window = (2, 2 * REACH * BLK, HD)
        scratch = [pltpu.VMEM(window, BF16), pltpu.VMEM(window, F32)]
        return grads(early_blocks, half, spans, (keys[1 - half], incoming), outs, then, after, scratch)

    ds_late_first, late_first, *spans = late(0, spans, (1, REACH), ())
    keys[1], rim = join(1, (late_first,))
    rim_first = to_inner(rim)
    ds_late_second, late_second, *spans = late(1, spans, (1, 0), (late_first,))
    ds_second, own_second, edge_second, *spans = early(1, spans, rim_second, (0, 0), (late_second,))
    back_first = to_outer(edge_second)
    ds_first, own_first, edge_first = early(0, spans, rim_first, None, (edge_second,))
    back_second = to_inner(edge_first)

    part = pltpu.VMEM(two_blocks.shape, BF16)
    d_query = call(
        functools.partial(finish_queries, heads),
        (starts, *keys, rim_second, rim_first, ds_late_first, ds_late_second, ds_second, ds_first),
        [shape(query.shape)],
        scratch=[part] * 4 + [pltpu.VMEM((2, 2 * REACH * BLK, HD), BF16), pltpu.SemaphoreType.DMA((4,))],
        limit=20,
        out_spec=HBM,
    )[0]

    d_keys, packed = (), ()
    for half, late_part, own_part, back, local in (
        (0, late_first, own_first, back_first, edge_second),
        (1, late_second, own_second, back_second, edge_first),
    ):
        packed = call(
            functools.partial(pack_grads, heads, half),
            (late_part, own_part, back, local),
            [block] * heads,
            scratch=[pltpu.VMEM((2, heads * BLK, HD), F32)],
            after=packed[:1],
        )
        inputs = (packed[0], *[swap(packed[t], t) for t in partners], *d_keys)
        d_keys = call(
            functools.partial(join_grads, heads, half),
            inputs,
            [shape(key.shape), shape(value.shape)],
            scratch=[pltpu.SemaphoreType.DMA((2 * heads,))],
            far=range(heads, len(inputs)),
            out_spec=HBM,
            aliases={heads + i: i for i in range(len(d_keys))},
        )
    d_key, d_value = d_keys
    return d_query, d_key, d_value


def solution(mesh):
    tokens = P("ctx", None, "head", None)
    columns = P("ctx", None, None, "head")
    return jax.shard_map(
        per_device,
        mesh=mesh,
        in_specs=(columns, tokens, tokens, columns, P()),
        out_specs=(columns, tokens, tokens),
        check_vma=False,
    )
```

```python
import functools

import jax
import jax.numpy as jnp
from jax import lax
from jax.experimental import pallas as pl
from jax.experimental.pallas import tpu as pltpu
from jax.sharding import PartitionSpec as P

HD = 128
BLK = 128
REACH = 2
SCALE = HD**-0.5
SCALE_LOG2E = SCALE * 1.4426950408889634
LATE = ((1, 1), (1, 2), (2, 1), (3, 1))
EARLY = ((2, 3), (3, 1))
BF16 = jnp.bfloat16
F32 = jnp.float32
VMEM = pl.BlockSpec(memory_space=pltpu.VMEM)
HBM = pl.BlockSpec(memory_space=pltpu.HBM)
ANY = pl.BlockSpec(memory_space=pl.ANY)


def shape(dims, dtype=BF16):
    return jax.ShapeDtypeStruct(dims, dtype)


def call(body, inputs, outs, scratch=(), flops=0, moved=0, limit=12, far=(), after=(), out_spec=VMEM, aliases=None):
    in_specs = [ANY] * len(after) + [
        HBM if i in far else VMEM for i in range(len(inputs))
    ]
    skip = len(after)
    name = body.func.__name__
    return pl.pallas_call(
        lambda *refs: body(*refs[skip:]),
        out_shape=outs,
        in_specs=in_specs,
        out_specs=[out_spec] * len(outs),
        scratch_shapes=list(scratch),
        input_output_aliases=aliases or {},
        compiler_params=pltpu.CompilerParams(vmem_limit_bytes=limit << 20),
        cost_estimate=pl.CostEstimate(flops=flops, bytes_accessed=moved, transcendentals=0),
        name=name,
    )(*after, *inputs)


def carry(pairs, sems):
    copies = [pltpu.make_async_copy(a, b, sems.at[i]) for i, (a, b) in enumerate(pairs)]
    for copy in copies:
        copy.start()
    for copy in copies:
        copy.wait()


def lanes(index):
    return pl.ds(pl.multiple_of(index * HD, HD), HD)


def rows(index, blocks=1):
    return pl.ds(pl.multiple_of(index * BLK, BLK), blocks * BLK)


def slot_of(half):
    odd = lax.rem(lax.axis_index("ctx"), 2)
    return 1 - odd if half == 0 else odd


def is_last():
    return lax.axis_index("ctx") == lax.axis_size("ctx") - 1


def span_of(half):
    ctx = lax.axis_index("ctx")
    return jnp.where(slot_of(half) == 0, ctx, 2 * lax.axis_size("ctx") - 1 - ctx)


def far_blocks(heads, half, key, value, sends):
    me = lax.axis_index("head")
    return [
        (array.at[0, slot_of(half), :, lanes(me ^ t)], sends[t - 2].at[i])
        for t in range(2, heads)
        for i, array in enumerate((key, value))
    ]


def close_blocks(t, key, value, there):
    me = lax.axis_index("head")
    return [
        (array.at[0, slot_of(half), :, lanes(me ^ t)], there.at[half, i])
        for half in range(2)
        for i, array in enumerate((key, value))
    ]


def pack_keys(heads, key, value, near, *refs):
    sends, sems = refs[:-1], refs[-1]
    carry(far_blocks(heads, 0, key, value, sends) + close_blocks(1, key, value, near), sems)


def fetch_rows(what, query, d_out, query_near, d_out_near, sems):
    half, first_block = what
    there = lambda array: array.at[0, slot_of(half), pl.ds(first_block * BLK, REACH * BLK), :]
    return [
        pltpu.make_async_copy(there(query), query_near, sems.at[0]),
        pltpu.make_async_copy(there(d_out), d_out_near, sems.at[1]),
    ]


def load_queries(heads, what, doc_start, key, value, query, d_out, starts_near, query_near, d_out_near, *refs):
    own, *sends, sems = refs
    pairs = far_blocks(heads, 1, key, value, sends) + close_blocks(0, key, value, own)
    pairs.append((doc_start, starts_near))
    copies = fetch_rows(what, query, d_out, query_near, d_out_near, sems)
    copies += [pltpu.make_async_copy(here, there, sems.at[2 + i]) for i, (here, there) in enumerate(pairs)]
    for copy in copies:
        copy.start()
    for copy in copies:
        copy.wait()


def while_fetching(what, body, inputs, refs):
    if what is None:
        return body(*inputs, *refs)
    query, d_out, *refs, sems = refs
    outs, near, scratch = refs[: what[2]], refs[what[2] : what[2] + 2], refs[what[2] + 2 :]
    copies = fetch_rows(what[:2], query, d_out, *near, sems)
    for copy in copies:
        copy.start()
    body(*inputs, *outs, *scratch)
    for copy in copies:
        copy.wait()


def join_keys(heads, half, own, near, *refs):
    parts, (span, rim) = refs[: heads - 2], refs[heads - 2 :]
    me = lax.axis_index("head")
    for t in range(heads):
        part = own.at[half] if t == 0 else near.at[half] if t == 1 else parts[t - 2]
        span[0, rows(me ^ t), :] = part[0]
        span[1, rows(me ^ t), :] = part[1]
    rim[...] = span[:, (heads - REACH) * BLK :, :]


def dot(a, b, ca, cb):
    return lax.dot_general(a, b, (((ca,), (cb,)), ((), ())), preferred_element_type=F32)


def products(task):
    n, first, queries, grads, keys, put = task
    count = queries.shape[1] // HD
    window = pl.ds(first * BLK, n * BLK)
    k, v = keys[0, window, :], keys[1, window, :]
    q = jnp.concatenate([queries[:, j * HD : (j + 1) * HD] for j in range(count)], axis=0)
    do = jnp.concatenate([grads[:, j * HD : (j + 1) * HD] for j in range(count)], axis=0)
    return k, q, do, dot(k, q, 1, 1), dot(v, do, 1, 1)


def weigh(task, k, q, do, s, dp):
    n = task[0]
    seen = lax.broadcasted_iota(jnp.int32, (BLK, BLK), 0) <= lax.broadcasted_iota(jnp.int32, (BLK, BLK), 1)
    hide = jnp.where(seen, 0.0, -jnp.inf)
    ps, dss = [], []
    for j in range(s.shape[1] // BLK):
        p_, ds_ = weigh_head(n, hide, s[:, j * BLK : (j + 1) * BLK], dp[:, j * BLK : (j + 1) * BLK])
        ps.append(p_)
        dss.append(ds_)
    return k, q, do, jnp.concatenate(ps, axis=1), jnp.concatenate(dss, axis=1)


def weigh_head(n, hide, s, dp):
    last = s[(n - 1) * BLK :] + hide
    return weigh_all(jnp.concatenate([s[: (n - 1) * BLK], last], axis=0) if n > 1 else last, dp)


def weigh_all(s, dp):
    peak = jnp.max(s, axis=0, keepdims=True)
    w = jnp.exp2((s - peak) * SCALE_LOG2E)
    inverse = 1.0 / jnp.sum(w, axis=0, keepdims=True)
    delta = jnp.sum(w * dp, axis=0, keepdims=True) * inverse
    p = w * inverse
    return p.astype(BF16), (p * (dp - delta)).astype(BF16)


def turn_back(k, ds):
    return (dot(k.T, ds, 1, 0) * SCALE).astype(BF16)


def put_queries(d_queries, k, ds):
    dq = turn_back(k, ds)
    for j in range(dq.shape[1] // BLK):
        d_queries[:, j * HD : (j + 1) * HD] = dq[:, j * BLK : (j + 1) * BLK].T


def gather(task, d_keys, k, q, do, p, ds):
    n, first, queries, grads, keys, put = task
    window = pl.ds(first * BLK, n * BLK)
    d_keys[0, window, :] += dot(ds, q, 1, 0) * SCALE
    d_keys[1, window, :] += dot(p, do, 1, 0)
    put(k, ds)


def pair_grads(a, b, d_keys):
    pa = products(a)
    wa = weigh(a, *pa)
    pb = products(b)
    gather(a, d_keys, *wa)
    wb = weigh(b, *pb)
    gather(b, d_keys, *wb)


def loose_grads(reach, visible, query, d_out, keys, put_loose, d_keys):
    group = 4
    steps = query.shape[1] // (group * HD)
    seen_rows = (reach + 1) * BLK

    def step(i, carried):
        b, g = i // steps, lax.rem(i, steps)
        window = rows(b + REACH - reach, reach + 1)
        columns = [lanes(g * group + j) for j in range(group)]
        q = jnp.concatenate([query[rows(b), c] for c in columns], axis=0)
        do = jnp.concatenate([d_out[rows(b), c] for c in columns], axis=0)
        k, v = keys[0, window, :], keys[1, window, :]
        count = jnp.where(b == 0, visible[0], visible[1])
        place = lax.broadcasted_iota(jnp.int32, (seen_rows, BLK), 0)
        token = lax.broadcasted_iota(jnp.int32, (seen_rows, BLK), 1)
        seen = (place >= (reach + 1 - count) * BLK) & (place - reach * BLK <= token)
        hide = jnp.where(seen, 0.0, -jnp.inf)
        s, dp = dot(k, q, 1, 1), dot(v, do, 1, 1)
        p, ds = weigh_all(s + jnp.concatenate([hide] * group, axis=1), dp)
        d_keys[0, window, :] += dot(ds, q, 1, 0) * SCALE
        d_keys[1, window, :] += dot(p, do, 1, 0)
        put_loose(b, columns, k, ds)
        return carried

    lax.fori_loop(0, 2 * steps, step, 0)


def visible_counts(per_span, half, first_block, doc_start):
    spot = lax.broadcasted_iota(jnp.int32, doc_start.shape, 1)
    marks = doc_start[...].astype(F32)
    visible = []
    for b in range(2):
        block = span_of(half) * per_span + first_block + b
        mark = jnp.sum(jnp.where(spot == block, 2 * marks, jnp.where(spot == block - 1, marks, 0.0)))
        visible.append(jnp.where(mark > 1.5, 1, jnp.where(mark > 0.5, 2, 3)))
    return visible


def span_part(fast, reach, first_block, per_span, half, doc_start, query, d_out, keys, put, put_loose, d_keys):
    d_keys[...] = jnp.zeros_like(d_keys)
    visible = visible_counts(per_span, half, first_block, doc_start)

    def task(b, n):
        return (
            n,
            b + REACH + 1 - n,
            query.at[pl.ds(b * BLK, BLK), :],
            d_out.at[pl.ds(b * BLK, BLK), :],
            keys,
            put(b),
        )

    common = [(n, then) for n in range(1, REACH + 2) for then in (1, n + 1) if then <= REACH + 1]
    common = [case for case in common if case in fast]
    chosen = False
    for n, then in common:
        here = (visible[0] == n) & (visible[1] == then)
        chosen = here | chosen

        @pl.when(here)
        def _(n=n, then=then):
            pair_grads(task(0, n), task(1, then), d_keys)

    @pl.when(jnp.logical_not(chosen))
    def _():
        loose_grads(reach, visible, query, d_out, keys, put_loose, d_keys)


def keepers(dscores):
    def put(b):
        def store(k, ds):
            dscores[b, : ds.shape[0], :] = ds

        return store

    def put_loose(b, columns, k, ds):
        for j, c in enumerate(columns):
            dscores[b, : ds.shape[0], c] = ds[:, j * BLK : (j + 1) * BLK]

    return put, put_loose


def late_blocks(per_span, half, what, doc_start, query, d_out, keys, *refs):
    def body(doc_start, query, d_out, keys, kept, d_keys):
        def put(b):
            return functools.partial(put_queries, kept.at[pl.ds(b * BLK, BLK), :])

        def put_loose(b, columns, k, ds):
            dq = turn_back(k, ds)
            for j, c in enumerate(columns):
                kept[rows(b), c] = dq[:, j * BLK : (j + 1) * BLK].T

        writers = (put, put_loose) if half == 0 else keepers(kept)
        span_part(LATE, REACH, REACH, per_span, half, doc_start, query, d_out, keys, *writers, d_keys)

    while_fetching(what, body, (doc_start, query, d_out, keys), refs)


def fill_window(per_span, half, window, keys, other, incoming):
    cut = REACH * BLK
    window[:, cut:, :] = keys[:, :cut, :]
    window[:, :cut, :] = incoming[...]
    if half == 1:

        @pl.when(is_last())
        def _():
            window[:, :cut, :] = other[:, (per_span - REACH) * BLK :, :]


def early_blocks(per_span, half, what, doc_start, query, d_out, keys, other, incoming, *refs):
    def body(doc_start, query, d_out, keys, other, incoming, dscores, d_own, d_rim, window, d_window):
        cut = REACH * BLK
        fill_window(per_span, half, window, keys, other, incoming)
        span_part(EARLY, REACH - 1, 0, per_span, half, doc_start, query, d_out, window, *keepers(dscores), d_window)
        d_rim[...] = d_window[:, :cut, :].astype(BF16)
        d_own[...] = d_window[:, cut:, :]

    while_fetching(what, body, (doc_start, query, d_out, keys, other, incoming), refs)


def finish_queries(per_span, doc_start, late_first, keys_0, keys_1, rim_second, rim_first, *refs):
    ds_late, ds_second, ds_first, d_query, part_late, part_second, part_first, window, sems = refs
    copies = []

    def send(part, half, first_block):
        there = d_query.at[0, slot_of(half), pl.ds(first_block * BLK, REACH * BLK), :]
        copies.append(pltpu.make_async_copy(part, there, sems.at[len(copies)]))
        copies[-1].start()

    def work_out(fast, reach, half, first_block, keys, dscores, part):
        visible = visible_counts(per_span, half, first_block, doc_start)

        def put(counts):
            for b, n in enumerate(counts):
                k = keys[0, (b + REACH + 1 - n) * BLK : (b + REACH + 1) * BLK, :]
                put_queries(part.at[pl.ds(b * BLK, BLK), :], k, dscores[b, : n * BLK, :])

        chosen = False
        for case in fast:
            here = (visible[0] == case[0]) & (visible[1] == case[1])
            chosen = here | chosen
            pl.when(here)(functools.partial(put, case))
        pl.when(jnp.logical_not(chosen))(functools.partial(put, (reach + 1, reach + 1)))
        send(part, half, first_block)

    send(late_first, 0, REACH)
    work_out(LATE, REACH, 1, REACH, keys_1, ds_late, part_late)
    fill_window(per_span, 1, window, keys_1, keys_0, rim_second)
    work_out(EARLY, REACH - 1, 1, 0, window, ds_second, part_second)
    fill_window(per_span, 0, window, keys_0, keys_1, rim_first)
    work_out(EARLY, REACH - 1, 0, 0, window, ds_first, part_first)
    for copy in copies:
        copy.wait()


def pack_grads(heads, half, late, own, back, local, *refs):
    sends, total = refs[:-1], refs[-1]
    me = lax.axis_index("head")
    cut = REACH * BLK
    total[...] = late[...]
    total[:, :cut, :] += own[...]
    total[:, (heads - REACH) * BLK :, :] += back[...].astype(F32)
    if half == 0:

        @pl.when(is_last())
        def _():
            total[:, (heads - REACH) * BLK :, :] += local[...].astype(F32)

    for t in range(heads):
        sends[t][...] = total[:, rows(me ^ t), :].astype(BF16)


def join_grads(heads, half, *refs):
    parts, (d_key, d_value, sems) = refs[:heads], refs[-3:]
    me = lax.axis_index("head")
    pairs = []
    for t in range(heads):
        for i, array in enumerate((d_key, d_value)):
            pairs.append((parts[t].at[i], array.at[0, slot_of(half), :, lanes(me ^ t)]))
    carry(pairs, sems)


def per_device(query, key, value, d_out, doc_start):
    ctx_count, heads = lax.axis_size("ctx"), lax.axis_size("head")
    block = shape((2, BLK, HD))
    partners = range(1, heads)
    swap = lambda x, t: lax.ppermute(x, "head", [(i, i ^ t) for i in range(heads)])
    outer = [p for i in range(1, ctx_count - 1, 2) for p in ((i, i + 1), (i + 1, i))]
    inner = [p for i in range(0, ctx_count, 2) for p in ((i, i + 1), (i + 1, i))]
    to_outer = lambda x: lax.ppermute(x, "ctx", outer)
    to_inner = lambda x: lax.ppermute(x, "ctx", inner)

    key, value, query, d_out = (
        pltpu.with_memory_space_constraint(x, pltpu.HBM) for x in (key, value, query, d_out)
    )
    both = shape((2, 2, BLK, HD))
    ready, *sends = call(
        functools.partial(pack_keys, heads),
        (key, value),
        [both] + [block] * (heads - 2),
        scratch=[pltpu.SemaphoreType.DMA((2 * heads,))],
        far=(0, 1),
    )
    near = swap(ready, 1)
    parts = [[swap(sends[t - 2], t) for t in range(2, heads)]]
    starts = pltpu.with_memory_space_constraint(doc_start[None], pltpu.HBM)
    two_blocks = shape((REACH * BLK, query.shape[3]))
    starts, *spans = call(
        functools.partial(load_queries, heads, (0, REACH)),
        (starts, key, value, query, d_out),
        [shape(starts.shape, jnp.int32), two_blocks, two_blocks, both] + [block] * (heads - 2),
        scratch=[pltpu.SemaphoreType.DMA((2 * heads + 3,))],
        moved=4 * query.size,
        far=range(5),
        after=(ready,),
    )
    spans, own, sends = spans[:2], spans[2], spans[3:]
    parts.append([swap(sends[t - 2], t) for t in range(2, heads)])

    def join(half, after):
        return call(
            functools.partial(join_keys, heads, half),
            (own, near, *parts[half]),
            [shape((2, heads * BLK, HD)), shape((2, REACH * BLK, HD))],
            after=after,
        )

    keys = [None, None]
    keys[0], rim = join(0, (spans[0],))
    rim_second = to_outer(rim)

    def grads(body, half, spans, more, outs, then, after, scratch=()):
        inputs = (starts, *spans, keys[half], *more)
        what = None
        if then is not None:
            what = (*then, len(outs))
            far = (len(inputs), len(inputs) + 1)
            inputs, outs = (*inputs, query, d_out), [*outs, two_blocks, two_blocks]
            scratch = [*scratch, pltpu.SemaphoreType.DMA((2,))]
        return call(
            functools.partial(body, heads, half, what),
            inputs,
            outs,
            scratch=scratch,
            far=() if what is None else far,
            limit=20,
            after=after,
        )

    dscores = shape((2, (REACH + 1) * BLK, query.shape[3]))

    def late(half, spans, then, after):
        outs = [two_blocks if half == 0 else dscores, shape((2, heads * BLK, HD), F32)]
        return grads(late_blocks, half, spans, (), outs, then, after)

    def early(half, spans, incoming, then, after):
        outs = [dscores, shape((2, REACH * BLK, HD), F32), shape((2, REACH * BLK, HD))]
        window = (2, 2 * REACH * BLK, HD)
        scratch = [pltpu.VMEM(window, BF16), pltpu.VMEM(window, F32)]
        return grads(early_blocks, half, spans, (keys[1 - half], incoming), outs, then, after, scratch)

    dq_late_first, late_first, *spans = late(0, spans, (1, REACH), ())
    keys[1], rim = join(1, (late_first,))
    rim_first = to_inner(rim)
    ds_late, late_second, *spans = late(1, spans, (1, 0), (late_first,))
    ds_second, own_second, edge_second, *spans = early(1, spans, rim_second, (0, 0), (late_second,))
    back_first = to_outer(edge_second)
    ds_first, own_first, edge_first = early(0, spans, rim_first, None, (edge_second,))
    back_second = to_inner(edge_first)

    part = pltpu.VMEM(two_blocks.shape, BF16)
    d_query = call(
        functools.partial(finish_queries, heads),
        (starts, dq_late_first, *keys, rim_second, rim_first, ds_late, ds_second, ds_first),
        [shape(query.shape)],
        scratch=[part] * 3 + [pltpu.VMEM((2, 2 * REACH * BLK, HD), BF16), pltpu.SemaphoreType.DMA((4,))],
        limit=20,
        out_spec=HBM,
    )[0]

    d_keys, packed = (), ()
    for half, late_part, own_part, back, local in (
        (0, late_first, own_first, back_first, edge_second),
        (1, late_second, own_second, back_second, edge_first),
    ):
        packed = call(
            functools.partial(pack_grads, heads, half),
            (late_part, own_part, back, local),
            [block] * heads,
            scratch=[pltpu.VMEM((2, heads * BLK, HD), F32)],
            after=packed[:1],
        )
        inputs = (packed[0], *[swap(packed[t], t) for t in partners], *d_keys)
        d_keys = call(
            functools.partial(join_grads, heads, half),
            inputs,
            [shape(key.shape), shape(value.shape)],
            scratch=[pltpu.SemaphoreType.DMA((2 * heads,))],
            far=range(heads, len(inputs)),
            out_spec=HBM,
            aliases={heads + i: i for i in range(len(d_keys))},
        )
    d_key, d_value = d_keys
    return d_query, d_key, d_value


def solution(mesh):
    tokens = P("ctx", None, "head", None)
    columns = P("ctx", None, None, "head")
    return jax.shard_map(
        per_device,
        mesh=mesh,
        in_specs=(columns, tokens, tokens, columns, P()),
        out_specs=(columns, tokens, tokens),
        check_vma=False,
    )
```
